128 devices in a mesh: section: 4 (over y), tp: 8 (over x, z_lo), dec: 4 (over z_hi, core).
Axes of the slice: x: 4, y: 4, z: 4 (z_hi: 2, z_lo: 2; z = z_hi * 2 + z_lo), core: 2. Of those that a mesh axis runs over, the one named last changes fastest.
Arguments:
- hidden_in: bfloat16 [4, 1024, 8192], P('section', ('dec', 'tp')), may hold values from -3 to 3
- attn_gain: float32 [4, 8192], P('section'), may hold values from 0.5 to 1.5
- q_weight: bfloat16 [4, 8192, 4096], P('section', None, 'tp'), may hold values from -0.0625 to 0.0625
- key_weight_matrix: bfloat16 [4, 8192, 1024], P('section', None, 'tp'), may hold values from -0.0625 to 0.0625
- value_weight_matrix: bfloat16 [4, 8192, 1024], P('section', None, 'tp'), may hold values from -0.0625 to 0.0625
- o_weight: bfloat16 [4, 4096, 8192], P('section', 'tp'), may hold values from -0.375 to 0.375
- kv_pool: bfloat16 [4, 640, 16, 8, 256], P('section', 'dec', None, 'tp'), may hold values from -384 to 384
- block_table: int32 [4, 4, 160], P('section', 'dec'), may hold values from 0 to 159, each once within a row
- request_len: int32 [4, 16], P('section', 'dec'), may hold values from 16 to 3407, as said below
- prefix_len: int32 [4, 16], P('section', 'dec'), may hold values from 480 to 640, as said below
- new_len: int32 [4, 16], P('section', 'dec'), may hold values from 16 to 208, as said below
- page_owner: int32 [4, 896, 1], P('section', 'dec'), may hold values from 0 to 127; in each aligned block of 224 rows (0 to 223, 224 to 447, ..., all dimensions but the last counted through in order) at most 3 rows name the same one
Outputs:
- passed: bfloat16 [4, 1024, 8192], P('section', ('dec', 'tp'))
- received_pages: bfloat16 [128, 128, 3, 16, 1, 256], P(('section', 'tp', 'dec'))
- received_tags: int32 [128, 128, 3], P(('section', 'tp', 'dec'))
The draws below stay inside these ranges and needn't reach their ends.
Inputs may be any that keep to these rules, and one draw needn't show every extreme that they name: `prefix_len`: a multiple of 16; some request has exactly 640. `new_len`: a multiple of 16; the 4 entries of one section and decode index sum to 256. `request_len`: at least prefix_len + new_len of the same request. `block_table`: for each section and decode index, every pool page once. `page_owner`: among the rows of one device, no owner is named more than 3 times.
All inputs are finite; a program needn't handle non-finite values.
Results may differ from the reference program's by a relative error of at most 0.02.
The reference program's roundings to bfloat16 on the way count: a program that leaves them out, or rounds other values in their place, can miss the bound.
Values may be sent and summed in bfloat16 or wider, within the bound.
No kernel may reach another device: no remote copies, remote signals or barrier semaphores. Data moves between devices by JAX's collectives and lax.ppermute only.
A program may use at most 128 MiB of HBM per device.

```python
import math
import jax
import jax.numpy as jnp
import numpy as np
from jax import lax

MODEL_WIDTH = 8192
QUERY_HEADS = 32
KEY_VALUE_HEADS = 8
HEAD_DIMENSION = 128
PAGE_TOKENS = 16
TOK = 256
REQ = 4
MAXB = 40
NB = 56
POOL_PAGES = 160
CAP = 3
TOKENS_S = 1024
N_SECTION = 4
N_TP = 8
N_DEC = 4
DEVICES = 128


def request_plan(key):
    key_prefix, key_cut, key_open, key_extra = jax.random.split(key, 4)
    groups = N_SECTION * N_DEC
    page_total = TOK // PAGE_TOKENS
    prefix_page_list = jax.random.randint(key_prefix, (groups, REQ), 3 * MAXB // 4, MAXB + 1).astype(jnp.int32)
    prefix_page_list = prefix_page_list.at[0, 0].set(MAXB)
    orders = jax.vmap(lambda sub_key: jax.random.permutation(sub_key, page_total - 1))(jax.random.split(key_cut, groups))
    cut_points = jnp.sort(orders[:, :REQ - 1] + 1, axis=1).astype(jnp.int32)
    cut_points = cut_points.at[0].set((jnp.arange(REQ - 1, dtype=jnp.int32) + page_total - REQ + 1).astype(jnp.int32))
    boundaries = jnp.concatenate([jnp.zeros((groups, 1), jnp.int32), cut_points, jnp.full((groups, 1), page_total, jnp.int32)], axis=1)
    fresh_pages = boundaries[:, 1:] - boundaries[:, :-1]
    open_flag = jax.random.randint(key_open, (groups, REQ), 0, 16) == 0
    open_flag = open_flag.at[0, 0].set(True)
    extra_tokens = jax.random.randint(key_extra, (groups, REQ), 1, 4 * PAGE_TOKENS * MAXB)
    extra_tokens = extra_tokens.at[0, 0].set(4 * PAGE_TOKENS * MAXB - 1)
    prefix_tokens = prefix_page_list * PAGE_TOKENS
    new_tokens = fresh_pages * PAGE_TOKENS
    full_length = prefix_tokens + new_tokens + jnp.where(open_flag, extra_tokens, 0)
    out_shape = (N_SECTION, N_DEC * REQ)
    return (full_length.reshape(out_shape).astype(jnp.int32), prefix_tokens.reshape(out_shape).astype(jnp.int32), new_tokens.reshape(out_shape).astype(jnp.int32))


def draw_request_len(key, part):
    return request_plan(key)[0]


def draw_prefix_len(key, part):
    return request_plan(key)[1]


def draw_new_len(key, part):
    return request_plan(key)[2]


def draw_kv_pool(key, part):
    key = jax.random.fold_in(key, 7)
    key_values = jax.random.fold_in(key, 0)
    pool_layout_shape = (N_SECTION, N_DEC * POOL_PAGES, PAGE_TOKENS, KEY_VALUE_HEADS, 2 * HEAD_DIMENSION)
    values = jnp.clip(jax.random.normal(key_values, pool_layout_shape, jnp.float32), -6.0, 6.0)
    return values.astype(jnp.bfloat16)


def block_levels(rng, shape, cuts, low, top_value):
    def one(position, shards_of):
        heights = jax.random.uniform(jax.random.fold_in(jax.random.fold_in(rng, 6), position), (shards_of,), jnp.float32, low / len(cuts), top_value / len(cuts))
        return jnp.repeat(jnp.exp(heights), shape[position] // shards_of).reshape((-1,) + (1,) * (len(shape) - position - 1))

    gain = one(*cuts[0])
    for cut in cuts[1:]:
        gain = gain * one(*cut)
    return gain


def shared_out(stream_key, own, number, rows, count, top, bound, slope):
    ranking = jax.random.permutation(stream_key, count)
    packed, common = load_shares(count, rows * top, bound, slope, True), load_shares(count, rows * top, bound, slope, False)
    places = jnp.arange(count)

    def named(lengths, rotation):
        used = int((lengths > 0).sum())
        fixed = max(1, used // 4)
        moved = fixed + (places - fixed + rotation * (used - fixed)) % max(1, count - fixed)
        return jnp.zeros((count,), jnp.int32).at[ranking[jnp.where(places < fixed, places, moved)]].set(jnp.asarray(lengths, jnp.int32))

    lengths = jnp.where(number % 4 == 0, named(packed, number // 4), named(common, number - number // 4 - 1))
    mixed = jax.random.permutation(jax.random.fold_in(own, 3), count)
    source_of, taker = mixed[0:count // 2 * 2:2], mixed[1:count // 2 * 2:2]
    margin = jnp.minimum(lengths[source_of] - 1, bound - lengths[taker]) // 2
    margin = jnp.where((source_of == ranking[0]) | (taker == ranking[0]) | (lengths[taker] == 0), 0, jnp.maximum(margin, 0))
    moved = jax.random.randint(jax.random.fold_in(own, 4), (count // 2,), 0, 1 << 20) % (margin + 1)
    lengths = lengths.at[source_of].add(-moved).at[taker].add(moved)
    members = jnp.searchsorted(jnp.cumsum(lengths), jnp.arange(rows * top), side="right").astype(jnp.int32)
    grid = members.reshape(top, rows).T
    grid = grid[jax.random.permutation(jax.random.fold_in(own, 1), rows)]
    rotation = jax.random.randint(jax.random.fold_in(own, 2), (rows, 1), 0, top)
    return jnp.take_along_axis(grid, (jnp.arange(top)[None, :] + rotation) % top, axis=1)


def load_shares(amount, total, most, slope, full):
    weights = [(1 << 20) // math.isqrt(grade ** slope) + 1 for grade in range(1, amount + 1)]
    largest = most if full else min(most, max(-(-total // amount), total * weights[0] // sum(weights)))
    least = 1 if total - largest >= amount - 1 else 0
    given, surplus = [largest] + [least] * (amount - 1), total - largest - least * (amount - 1)
    while surplus > 0:
        movable = [i for i in range(1, amount) if given[i] < largest] or [i for i in range(1, amount) if given[i] < most]
        whole, remaining = sum([weights[i] for i in movable]), surplus
        for i in movable:
            addition = min(most - given[i], max(1, remaining * weights[i] // whole), surplus)
            given[i] = given[i] + addition
            surplus = surplus - addition
    return np.array(given)


def scatter_about(key, dims, width, reach, pieces=(), kind=jnp.bfloat16):
    drawn = width * jax.random.normal(key, dims, jnp.float32)
    if pieces:
        drawn = drawn * block_levels(key, dims, pieces, -0.22, 0.18)
    return jnp.clip(drawn, -reach, reach).astype(kind)


def setup_inputs(seed: int = 0) -> dict:
    key_list = jax.random.split(jax.random.key(seed), 13)
    hidden_in = scatter_about(key_list[0], (N_SECTION, TOKENS_S, MODEL_WIDTH), 0.5, 3.0, ((0, 4), (1, 32)))
    attn_gain = jnp.clip(1.0 + 0.1 * jax.random.normal(key_list[1], (N_SECTION, MODEL_WIDTH), jnp.float32), 0.5, 1.5)
    q_weight = scatter_about(key_list[2], (N_SECTION, MODEL_WIDTH, QUERY_HEADS * HEAD_DIMENSION), MODEL_WIDTH ** -0.5, 0.0625, ((0, 4), (2, 8)))
    key_weight_matrix = scatter_about(key_list[3], (N_SECTION, MODEL_WIDTH, KEY_VALUE_HEADS * HEAD_DIMENSION), MODEL_WIDTH ** -0.5, 0.0625, ((0, 4), (2, 8)))
    value_weight_matrix = scatter_about(key_list[4], (N_SECTION, MODEL_WIDTH, KEY_VALUE_HEADS * HEAD_DIMENSION), MODEL_WIDTH ** -0.5, 0.0625, ((0, 4), (2, 8)))
    o_weight = scatter_about(key_list[5], (N_SECTION, QUERY_HEADS * HEAD_DIMENSION, MODEL_WIDTH), (QUERY_HEADS * HEAD_DIMENSION // 16) ** -0.5, 0.375, ((0, 4), (1, 8)))
    kv_pool = draw_kv_pool(jax.random.fold_in(key_list[12], 71), 0)
    block_table = jax.vmap(lambda own: jax.random.permutation(own, POOL_PAGES))(jax.random.split(key_list[7], N_SECTION * N_DEC)).reshape((N_SECTION, N_DEC, POOL_PAGES)).astype(jnp.int32)
    request_len = draw_request_len(jax.random.fold_in(key_list[12], 71), 0)
    prefix_len = draw_prefix_len(jax.random.fold_in(key_list[12], 71), 0)
    new_len = draw_new_len(jax.random.fold_in(key_list[12], 71), 0)
    page_owner_keys = jax.random.split(jax.random.fold_in(key_list[11], 1), N_SECTION * (N_DEC * REQ * NB) // (REQ * NB))
    page_owner_turns = jax.random.permutation(jax.random.fold_in(key_list[11], 3), N_SECTION * (N_DEC * REQ * NB) // (REQ * NB))
    page_owner = jax.vmap(lambda own, number: shared_out(jax.random.fold_in(key_list[11], 2), own, number, REQ * NB, DEVICES, 1, CAP, 2))(page_owner_keys, page_owner_turns).reshape((N_SECTION, N_DEC * REQ * NB, 1))
    return {"hidden_in": hidden_in, "attn_gain": attn_gain, "q_weight": q_weight, "key_weight_matrix": key_weight_matrix, "value_weight_matrix": value_weight_matrix, "o_weight": o_weight, "kv_pool": kv_pool, "block_table": block_table, "request_len": request_len, "prefix_len": prefix_len, "new_len": new_len, "page_owner": page_owner}


theta_base = 500000.0
eps_norm = 1e-05
neg_large = -1e+30

def rotary_embedding(values, token_positions, head_size):
    half_size = head_size // 2
    frequency = theta_base ** (-(jnp.arange(half_size, dtype=jnp.float32) * 2.0) / head_size)
    angles = token_positions.astype(jnp.float32)[:, None] * frequency[None, :]
    cosine = jnp.cos(angles)[:, None, :]
    sine_part = jnp.sin(angles)[:, None, :]
    first_half = values[..., :half_size]
    second = values[..., half_size:]
    return jnp.concatenate([first_half * cosine - second * sine_part, second * cosine + first_half * sine_part], axis=-1)

def token_layout(prefix, new_tokens, token_batch):
    new_ends = jnp.cumsum(new_tokens).astype(jnp.int32)
    new_starts = (new_ends - new_tokens).astype(jnp.int32)
    token_index = jnp.arange(token_batch, dtype=jnp.int32)
    token_req = lax.optimization_barrier(jnp.sum((token_index[:, None] >= new_ends[None, :]).astype(jnp.int32), axis=1)).astype(jnp.int32)
    membership = token_req[:, None] == jnp.arange(new_tokens.shape[0], dtype=jnp.int32)[None, :]
    own_prefix = lax.optimization_barrier(jnp.sum(jnp.where(membership, prefix[None, :], 0), axis=1)).astype(jnp.int32)
    own_start = lax.optimization_barrier(jnp.sum(jnp.where(membership, new_starts[None, :], 0), axis=1)).astype(jnp.int32)
    token_positions = (own_prefix + token_index - own_start).astype(jnp.int32)
    return (token_req, token_positions, new_starts, own_prefix)

def attention_mask(token_req, own_prefix, prefix_slots, token_batch):
    slot_number = jnp.arange(prefix_slots, dtype=jnp.int32)
    slot_req = slot_number // (MAXB * PAGE_TOKENS)
    slot_pos = slot_number % (MAXB * PAGE_TOKENS)
    prefix_ok = (slot_req[None, :] == token_req[:, None]) & (slot_pos[None, :] < own_prefix[:, None])
    token_index = jnp.arange(token_batch, dtype=jnp.int32)
    recent_ok = (token_req[None, :] == token_req[:, None]) & (token_index[None, :] <= token_index[:, None])
    return jnp.concatenate([prefix_ok, recent_ok], axis=1)

def apply_attention(query_rows_all, key_row_values, value_row_values, permitted_mask):
    scores = jnp.einsum('tkgd,skd->kgts', query_rows_all.astype(jnp.float32), key_row_values.astype(jnp.float32)) / math.sqrt(query_rows_all.shape[-1])
    scores = jnp.where(permitted_mask[None, None], scores, neg_large)
    row_max = lax.optimization_barrier(jnp.max(scores, axis=-1, keepdims=True))
    exp_scores = jnp.exp(scores - row_max)
    probabilities = (exp_scores / lax.optimization_barrier(jnp.sum(exp_scores, axis=-1, keepdims=True))).astype(jnp.bfloat16)
    mixed_heads = jnp.einsum('kgts,skd->tkgd', probabilities.astype(jnp.float32), value_row_values.astype(jnp.float32))
    return mixed_heads.astype(jnp.bfloat16)

def collect_pages(prefix_page_list, fresh_pages, prefix, new_tokens, full_length, new_starts):
    request_number = jnp.arange(prefix.shape[0], dtype=jnp.int32)[:, None]
    block_number = jnp.arange(NB, dtype=jnp.int32)[None, :]
    prefix_count = (prefix // PAGE_TOKENS).astype(jnp.int32)[:, None]
    new_count = (new_tokens // PAGE_TOKENS).astype(jnp.int32)[:, None]
    page_base = (new_starts // PAGE_TOKENS).astype(jnp.int32)[:, None]
    from_prefix = block_number < prefix_count
    new_index = jnp.clip(page_base + block_number - prefix_count, 0, fresh_pages.shape[0] - 1)
    source_row = jnp.where(from_prefix, request_number * MAXB + jnp.minimum(block_number, MAXB - 1), prefix_page_list.shape[0] + new_index).reshape(-1).astype(jnp.int32)
    exists = block_number < prefix_count + new_count
    finished = (full_length == prefix + new_tokens)[:, None]
    sent_flag = (exists & finished).reshape(-1)
    sources = jnp.concatenate([prefix_page_list, fresh_pages], axis=0)
    return (sources[source_row], sent_flag)

def place_pages(pages, owner_list, sent_flag, devices, capacity):
    row_total = owner_list.shape[0]
    owner_hits = ((owner_list[:, None] == jnp.arange(devices, dtype=jnp.int32)[None, :]) & sent_flag[:, None]).astype(jnp.int32)
    earlier = (jnp.cumsum(owner_hits, axis=0) - owner_hits).astype(jnp.int32)
    slot_index = lax.optimization_barrier(jnp.sum(earlier * owner_hits, axis=1)).astype(jnp.int32)
    target = jnp.where(sent_flag, owner_list, devices).astype(jnp.int32)
    page_buffer = jnp.zeros((devices, capacity) + pages.shape[1:], pages.dtype).at[target, slot_index].set(pages, mode='drop')
    page_tags = jnp.zeros((devices, capacity), jnp.int32).at[target, slot_index].set(jnp.arange(row_total, dtype=jnp.int32) + 1, mode='drop')
    return (page_buffer, page_tags)

def group_step(row_block, norm_gain, q_proj, key_projection, value_projection, o_proj, pool_pages, block_ids, prefix, new_tokens, full_length):
    token_batch = row_block.shape[0]
    rows_float = row_block.astype(jnp.float32)
    normalized_hidden = (rows_float * lax.rsqrt(lax.optimization_barrier(jnp.mean(rows_float * rows_float, axis=-1, keepdims=True)) + eps_norm) * norm_gain).astype(jnp.bfloat16)
    token_req, token_positions, new_starts, own_prefix = token_layout(prefix, new_tokens, token_batch)
    query_rows_all = rotary_embedding(jnp.dot(normalized_hidden, q_proj, preferred_element_type=jnp.float32).reshape(token_batch, QUERY_HEADS, HEAD_DIMENSION), token_positions, HEAD_DIMENSION).astype(jnp.bfloat16)
    fresh_keys = rotary_embedding(jnp.dot(normalized_hidden, key_projection, preferred_element_type=jnp.float32).reshape(token_batch, KEY_VALUE_HEADS, HEAD_DIMENSION), token_positions, HEAD_DIMENSION).astype(jnp.bfloat16)
    fresh_values = jnp.dot(normalized_hidden, value_projection, preferred_element_type=jnp.float32).astype(jnp.bfloat16).reshape(token_batch, KEY_VALUE_HEADS, HEAD_DIMENSION)
    prefix_page_list = pool_pages[block_ids]
    flattened_prefix = prefix_page_list.reshape(-1, KEY_VALUE_HEADS, 2 * HEAD_DIMENSION)
    key_row_values = jnp.concatenate([flattened_prefix[:, :, :HEAD_DIMENSION], fresh_keys], axis=0)
    value_row_values = jnp.concatenate([flattened_prefix[:, :, HEAD_DIMENSION:], fresh_values], axis=0)
    permitted_mask = attention_mask(token_req, own_prefix, flattened_prefix.shape[0], token_batch)
    attention_output = apply_attention(query_rows_all.reshape(token_batch, KEY_VALUE_HEADS, QUERY_HEADS // KEY_VALUE_HEADS, HEAD_DIMENSION), key_row_values, value_row_values, permitted_mask).reshape(token_batch, QUERY_HEADS * HEAD_DIMENSION)
    col_width = QUERY_HEADS * HEAD_DIMENSION // N_TP
    head_total = jnp.zeros((token_batch, MODEL_WIDTH), jnp.float32)
    for tp_index in range(N_TP):
        head_part = jnp.dot(attention_output[:, tp_index * col_width:(tp_index + 1) * col_width], o_proj[tp_index * col_width:(tp_index + 1) * col_width], preferred_element_type=jnp.float32)
        head_total = head_total + lax.optimization_barrier(head_part.astype(jnp.bfloat16)).astype(jnp.float32)
    mixed_rows = (rows_float + head_total).astype(jnp.bfloat16)
    fresh_pages = jnp.concatenate([fresh_keys, fresh_values], axis=-1).reshape(token_batch // PAGE_TOKENS, PAGE_TOKENS, KEY_VALUE_HEADS, 2 * HEAD_DIMENSION)
    pages, sent_flag = collect_pages(prefix_page_list, fresh_pages, prefix, new_tokens, full_length, new_starts)
    return (mixed_rows, pages, sent_flag)

def reference(hidden_in, attn_gain, q_weight, key_weight_matrix, value_weight_matrix, o_weight, kv_pool, block_table, request_len, prefix_len, new_len, page_owner):
    key_value_heads = KEY_VALUE_HEADS // N_TP
    section_rows, section_pages, section_tags = ([], [], [])
    for section_index in range(N_SECTION):
        dec_rows, dec_pages, dec_tags = ([], [], [])
        for group_index in range(N_DEC):
            row_block = hidden_in[section_index, group_index * TOK:(group_index + 1) * TOK]
            pool_pages = kv_pool[section_index, group_index * POOL_PAGES:(group_index + 1) * POOL_PAGES]
            first_req = group_index * REQ
            prefix = prefix_len[section_index, first_req:first_req + REQ]
            new_tokens = new_len[section_index, first_req:first_req + REQ]
            full_length = request_len[section_index, first_req:first_req + REQ]
            owner_list = page_owner[section_index, first_req * NB:(first_req + REQ) * NB, 0]
            mixed_rows, pages, sent_flag = group_step(row_block, attn_gain[section_index].astype(jnp.float32), q_weight[section_index], key_weight_matrix[section_index], value_weight_matrix[section_index], o_weight[section_index], pool_pages, block_table[section_index, group_index], prefix, new_tokens, full_length)
            page_buffer, page_tags = place_pages(pages, owner_list, sent_flag, DEVICES, CAP)
            page_buffer = page_buffer.reshape(DEVICES, CAP, PAGE_TOKENS, N_TP, key_value_heads, 2 * HEAD_DIMENSION)
            dec_pages.append(jnp.moveaxis(page_buffer, 3, 0))
            dec_tags.append(jnp.broadcast_to(page_tags[None], (N_TP, DEVICES, CAP)))
            dec_rows.append(mixed_rows)
        section_rows.append(jnp.concatenate(dec_rows, axis=0))
        section_pages.append(jnp.stack(dec_pages, axis=1))
        section_tags.append(jnp.stack(dec_tags, axis=1))
    passed = jnp.roll(jnp.stack(section_rows, axis=0), 1, axis=0)
    sent_all = jnp.stack(section_pages, axis=0).reshape(DEVICES, DEVICES, CAP, PAGE_TOKENS, key_value_heads, 2 * HEAD_DIMENSION)
    received_pages = jnp.swapaxes(sent_all, 0, 1)
    tags_all = jnp.stack(section_tags, axis=0).reshape(DEVICES, DEVICES, CAP)
    received_tags = jnp.swapaxes(tags_all, 0, 1)
    return (passed, received_pages, received_tags)
```

```python
import functools
import math

import jax
import jax.numpy as jnp
from jax import lax
from jax.experimental import pallas as pl
from jax.experimental.pallas import tpu as pltpu
from jax.sharding import PartitionSpec as P

HEAD_DIMENSION = 128
PAGE_TOKENS = 16
MAXB = 40
NB = 56
CAP = 3
ROWS = 32

theta_base = 500000.0
eps_norm = 1e-05
neg_large = -1e30

MIB = 1 << 20
VMEM = pl.BlockSpec(memory_space=pltpu.VMEM)
SMEM = pl.BlockSpec(memory_space=pltpu.SMEM)
ANY = pl.BlockSpec(memory_space=pl.ANY)

PIECES = ((0, 0), (0, 1), (1, 0), (3, 0), (1, 1), (3, 1), (2, 0), (2, 1))


def tp_route(dx, dz, n_tp):
    nx = n_tp // 2
    return [(x * 2 + z, ((x + dx) % nx) * 2 + (z ^ dz)) for x in range(nx) for z in range(2)]


def send(block, dx, dz):
    return lax.ppermute(block, "tp", tp_route(dx, dz, lax.axis_size("tp")))


def shifted(block, axis, distance):
    count = lax.axis_size(axis)
    return lax.ppermute(block, axis, [((i - distance) % count, i) for i in range(count)])


def norm_kernel(x_ref, gain_ref, out_ref):
    x = x_ref[...].astype(jnp.float32)
    scale = lax.rsqrt(jnp.mean(x * x, axis=-1, keepdims=True) + eps_norm)
    out_ref[...] = (x * scale * gain_ref[...]).astype(jnp.bfloat16)


def normalize(x, gain):
    return pl.pallas_call(
        norm_kernel,
        out_shape=jax.ShapeDtypeStruct(x.shape, jnp.bfloat16),
        in_specs=[VMEM, VMEM],
        out_specs=VMEM,
        compiler_params=pltpu.CompilerParams(vmem_limit_bytes=16 * MIB),
        cost_estimate=pl.CostEstimate(flops=4 * x.size, bytes_accessed=4 * x.size, transcendentals=0),
        name="norm",
    )(x, gain)


def qkv_kernel(order, *refs):
    pieces = refs[:8]
    wq, wk, wv, cos_ref, sin_ref, q_ref, kv_ref, acc_q, acc_kv = refs[8:]
    step = pl.program_id(0)

    @pl.when(step == 0)
    def _():
        acc_q[...] = jnp.zeros_like(acc_q)
        acc_kv[...] = jnp.zeros_like(acc_kv)

    x = jnp.concatenate([p[...] for p in pieces], axis=0)
    wkv = jnp.concatenate([wk[...], wv[...]], axis=1)
    acc_q[...] += jnp.dot(x, wq[...], preferred_element_type=jnp.float32)
    acc_kv[...] += jnp.dot(x, wkv, preferred_element_type=jnp.float32)

    @pl.when(step == pl.num_programs(0) - 1)
    def _():
        heads = acc_q.shape[1] // HEAD_DIMENSION
        for p in range(8):
            rows = pl.ds(pl.multiple_of(order[p] * ROWS, ROWS), ROWS)
            cos = cos_ref[rows, :]
            sin = sin_ref[rows, :]
            here = slice(p * ROWS, (p + 1) * ROWS)

            def rotate(v):
                return v * cos + pltpu.roll(v, HEAD_DIMENSION // 2, 1) * sin

            for h in range(heads):
                cols = slice(h * HEAD_DIMENSION, (h + 1) * HEAD_DIMENSION)
                q_ref[rows, cols] = rotate(acc_q[here, cols]).astype(jnp.bfloat16)
            kv_ref[rows, :HEAD_DIMENSION] = rotate(acc_kv[here, :HEAD_DIMENSION]).astype(jnp.bfloat16)
            kv_ref[rows, HEAD_DIMENSION:] = acc_kv[here, HEAD_DIMENSION:].astype(jnp.bfloat16)


def project(order, pieces, wq, wk, wv, cos, sin):
    depth = wq.shape[0]
    block = 1024
    tokens = 8 * ROWS
    n_q, n_kv = wq.shape[1], wk.shape[1] + wv.shape[1]
    grid_spec = pltpu.PrefetchScalarGridSpec(
        num_scalar_prefetch=1,
        grid=(depth // block,),
        in_specs=[pl.BlockSpec((ROWS, block), lambda k, o: (0, k))] * 8
        + [
            pl.BlockSpec((block, n_q), lambda k, o: (k, 0)),
            pl.BlockSpec((block, wk.shape[1]), lambda k, o: (k, 0)),
            pl.BlockSpec((block, wv.shape[1]), lambda k, o: (k, 0)),
            pl.BlockSpec((tokens, HEAD_DIMENSION), lambda k, o: (0, 0)),
            pl.BlockSpec((tokens, HEAD_DIMENSION), lambda k, o: (0, 0)),
        ],
        out_specs=[
            pl.BlockSpec((tokens, n_q), lambda k, o: (0, 0)),
            pl.BlockSpec((tokens, n_kv), lambda k, o: (0, 0)),
        ],
        scratch_shapes=[
            pltpu.VMEM((tokens, n_q), jnp.float32),
            pltpu.VMEM((tokens, n_kv), jnp.float32),
        ],
    )
    return pl.pallas_call(
        qkv_kernel,
        grid_spec=grid_spec,
        out_shape=[
            jax.ShapeDtypeStruct((tokens, n_q), jnp.bfloat16),
            jax.ShapeDtypeStruct((tokens, n_kv), jnp.bfloat16),
        ],
        compiler_params=pltpu.CompilerParams(vmem_limit_bytes=24 * MIB),
        cost_estimate=pl.CostEstimate(
            flops=2 * tokens * depth * (n_q + n_kv),
            bytes_accessed=2 * depth * (n_q + n_kv + tokens),
            transcendentals=0,
        ),
        name="qkv",
    )(order, *pieces, wq, wk, wv, cos, sin)


def pages_kernel(take_ref, table_ref, pool_ref, buffer_ref, prefix_ref):
    def fill(i, _):
        row = take_ref[i]
        page = pool_ref[jnp.maximum(row, 0)]
        buffer_ref[i] = jnp.where(row >= 0, page, jnp.zeros_like(page))
        return 0

    lax.fori_loop(0, buffer_ref.shape[0], fill, 0, unroll=8)

    def gather(i, _):
        prefix_ref[i] = pool_ref[table_ref[i]]
        return 0

    lax.fori_loop(0, prefix_ref.shape[0], gather, 0, unroll=8)


def build_pages(take, table, pool):
    slots = take.shape[0]
    return pl.pallas_call(
        pages_kernel,
        out_shape=[
            jax.ShapeDtypeStruct((slots,) + pool.shape[1:], pool.dtype),
            jax.ShapeDtypeStruct((table.shape[0],) + pool.shape[1:], pool.dtype),
        ],
        in_specs=[SMEM, SMEM, VMEM],
        out_specs=[VMEM, VMEM],
        compiler_params=pltpu.CompilerParams(vmem_limit_bytes=24 * MIB),
        cost_estimate=pl.CostEstimate(flops=0, bytes_accessed=6 * MIB, transcendentals=0),
        name="pages",
    )(take, table, pool)


def patch_kernel(place_ref, fresh_ref, buffer_ref, out_ref, sems):
    del buffer_ref
    count = fresh_ref.shape[0]
    slots = out_ref.shape[0]

    def copy(i):
        return pltpu.make_async_copy(
            fresh_ref.at[i], out_ref.at[jnp.minimum(place_ref[i], slots - 1)], sems.at[i]
        )

    for i in range(count):
        @pl.when(place_ref[i] < slots)
        def _():
            copy(i).start()

    for i in range(count):
        @pl.when(place_ref[i] < slots)
        def _():
            copy(i).wait()


def patch_pages(place, fresh, buffer):
    return pl.pallas_call(
        patch_kernel,
        out_shape=jax.ShapeDtypeStruct(buffer.shape, buffer.dtype),
        in_specs=[SMEM, VMEM, ANY],
        out_specs=ANY,
        scratch_shapes=[pltpu.SemaphoreType.DMA((fresh.shape[0],))],
        input_output_aliases={2: 0},
        compiler_params=pltpu.CompilerParams(vmem_limit_bytes=8 * MIB),
        cost_estimate=pl.CostEstimate(flops=0, bytes_accessed=4 * fresh.size, transcendentals=0),
        name="patch",
    )(place, fresh, buffer)


TILE = 64


def attention_kernel(order_ref, ends_ref, prefix_len_ref, q_ref, kv_ref, prefix_ref, out_ref, q_s, o_s):
    tokens = q_ref.shape[0]
    heads = q_ref.shape[1] // HEAD_DIMENSION
    tiles = tokens // TILE
    requests = ends_ref.shape[0]
    slots = MAXB * PAGE_TOKENS
    for j in range(tiles):
        for h in range(heads):
            q_s[j, h * TILE : (h + 1) * TILE, :] = q_ref[
                j * TILE : (j + 1) * TILE, h * HEAD_DIMENSION : (h + 1) * HEAD_DIMENSION
            ]
    scale = 1.0 / math.sqrt(HEAD_DIMENSION)
    nt = (((1,), (1,)), ((), ()))

    def body(i, _):
        j, r = i // requests, i % requests
        end = ends_ref[r]
        start = jnp.where(r == 0, 0, ends_ref[jnp.maximum(r - 1, 0)])

        @pl.when((start < (j + 1) * TILE) & (end > j * TILE))
        def _():
            q = q_s[j]
            rows = pl.ds(pl.multiple_of(r * slots, slots), slots)
            s1 = lax.dot_general(
                q, prefix_ref[rows, :HEAD_DIMENSION], nt, preferred_element_type=jnp.float32
            )
            s2 = lax.dot_general(
                q, kv_ref[:, :HEAD_DIMENSION], nt, preferred_element_type=jnp.float32
            )
            slot = lax.broadcasted_iota(jnp.int32, s1.shape, 1)
            s1 = jnp.where(slot < prefix_len_ref[r], s1 * scale, neg_large)
            token = j * TILE + lax.rem(lax.broadcasted_iota(jnp.int32, s2.shape, 0), TILE)
            key = lax.broadcasted_iota(jnp.int32, s2.shape, 1)
            s2 = jnp.where((key >= start) & (key <= token), s2 * scale, neg_large)
            top = jnp.maximum(
                jnp.max(s1, axis=1, keepdims=True), jnp.max(s2, axis=1, keepdims=True)
            )
            p1 = jnp.exp(s1 - top)
            p2 = jnp.exp(s2 - top)
            total = jnp.sum(p1, axis=1, keepdims=True) + jnp.sum(p2, axis=1, keepdims=True)
            inverse = 1.0 / total
            o = jnp.dot(
                (p1 * inverse).astype(jnp.bfloat16),
                prefix_ref[rows, HEAD_DIMENSION:],
                preferred_element_type=jnp.float32,
            ) + jnp.dot(
                (p2 * inverse).astype(jnp.bfloat16),
                kv_ref[:, HEAD_DIMENSION:],
                preferred_element_type=jnp.float32,
            )
            own = j * TILE + lax.rem(lax.broadcasted_iota(jnp.int32, o.shape, 0), TILE)
            mine = (own >= start) & (own < end)
            o_s[j] = jnp.where(mine, o, o_s[j])

        return 0

    lax.fori_loop(0, tiles * requests, body, 0)
    per_tile = TILE // ROWS
    for p in range(8):
        at = order_ref[p]
        tile, part = at // per_tile, at % per_tile
        for h in range(heads):
            out_ref[p * ROWS : (p + 1) * ROWS, h * HEAD_DIMENSION : (h + 1) * HEAD_DIMENSION] = o_s[
                tile, pl.ds(pl.multiple_of(h * TILE + part * ROWS, ROWS), ROWS), :
            ].astype(jnp.bfloat16)


def attend(order, ends, prefix_len, q, kv, prefix):
    tokens, width = q.shape
    heads = width // HEAD_DIMENSION
    work = 2 * tokens * heads * (MAXB * PAGE_TOKENS + tokens) * HEAD_DIMENSION * 2 * 2
    return pl.pallas_call(
        attention_kernel,
        out_shape=jax.ShapeDtypeStruct((tokens, width), jnp.bfloat16),
        in_specs=[SMEM, SMEM, SMEM, VMEM, VMEM, VMEM],
        out_specs=VMEM,
        scratch_shapes=[
            pltpu.VMEM((tokens // TILE, heads * TILE, HEAD_DIMENSION), jnp.bfloat16),
            pltpu.VMEM((tokens // TILE, heads * TILE, HEAD_DIMENSION), jnp.float32),
        ],
        compiler_params=pltpu.CompilerParams(vmem_limit_bytes=24 * MIB),
        cost_estimate=pl.CostEstimate(
            flops=work, bytes_accessed=3 * MIB, transcendentals=2 * tokens * heads * 896
        ),
        name="attention",
    )(order, ends, prefix_len, q, kv, prefix)


def out_kernel(x_ref, w_ref, *outs):
    y = jnp.dot(x_ref[...], w_ref[...], preferred_element_type=jnp.float32).astype(jnp.bfloat16)
    for p in range(8):
        outs[p][...] = y[p * ROWS : (p + 1) * ROWS]


def out_project(x, w):
    tokens, depth = x.shape
    width = w.shape[1]
    block = 1024
    return pl.pallas_call(
        out_kernel,
        grid=(width // block,),
        in_specs=[
            pl.BlockSpec((tokens, depth), lambda n: (0, 0)),
            pl.BlockSpec((depth, block), lambda n: (0, n)),
        ],
        out_specs=[pl.BlockSpec((ROWS, block), lambda n: (0, n))] * 8,
        out_shape=[jax.ShapeDtypeStruct((ROWS, width), jnp.bfloat16)] * 8,
        compiler_params=pltpu.CompilerParams(vmem_limit_bytes=16 * MIB),
        cost_estimate=pl.CostEstimate(
            flops=2 * tokens * depth * width,
            bytes_accessed=2 * (depth * width + tokens * width),
            transcendentals=0,
        ),
        name="out",
    )(x, w)


def token_tables(prefix, new_tokens, new_ends, tokens):
    new_starts = new_ends - new_tokens
    index = jnp.arange(tokens, dtype=jnp.int32)
    request = jnp.sum((index[:, None] >= new_ends[None, :]).astype(jnp.int32), axis=1)
    member = request[:, None] == jnp.arange(new_tokens.shape[0], dtype=jnp.int32)[None, :]
    position = index + jnp.sum(jnp.where(member, (prefix - new_starts)[None, :], 0), axis=1)
    half = HEAD_DIMENSION // 2
    frequency = theta_base ** (-(jnp.arange(half, dtype=jnp.float32) * 2.0) / HEAD_DIMENSION)
    angles = position.astype(jnp.float32)[:, None] * frequency[None, :]
    cosine, sine = jnp.cos(angles), jnp.sin(angles)
    return (
        jnp.concatenate([cosine, cosine], axis=1),
        jnp.concatenate([-sine, sine], axis=1),
    )


def page_plan(prefix, new_tokens, new_ends, full_length, table, owners, devices, fresh_count):
    requests = prefix.shape[0]
    prefix_count = (prefix // PAGE_TOKENS)[:, None]
    new_count = (new_tokens // PAGE_TOKENS)[:, None]
    page_base = ((new_ends - new_tokens) // PAGE_TOKENS)[:, None]
    block = jnp.arange(NB, dtype=jnp.int32)[None, :]
    request = jnp.arange(requests, dtype=jnp.int32)[:, None]
    from_prefix = block < prefix_count
    exists = block < prefix_count + new_count
    finished = (full_length == prefix + new_tokens)[:, None]
    sent = (exists & finished).reshape(-1)
    target = jnp.where(sent, owners, devices)
    rows = target.shape[0]
    row = jnp.arange(rows, dtype=jnp.int32)
    rank = jnp.sum(
        ((target[:, None] == target[None, :]) & (row[None, :] < row[:, None])).astype(jnp.int32),
        axis=1,
    )
    code = jnp.where(sent, target * CAP + rank, devices * CAP)
    place = jnp.arange(devices * CAP, dtype=jnp.int32)
    hit = code[:, None] == place[None, :]
    tags = jnp.sum(jnp.where(hit, row[:, None] + 1, 0), axis=0)
    padded = jnp.pad(table.reshape(requests, MAXB), ((0, 0), (0, NB - MAXB)))
    source = jnp.where(from_prefix, padded, -1).reshape(-1)
    take = jnp.sum(jnp.where(hit, source[:, None] + 1, 0), axis=0) - 1
    fresh_of = jnp.where(exists & ~from_prefix, page_base + block - prefix_count, -1).reshape(-1)
    number = jnp.arange(fresh_count, dtype=jnp.int32)
    fresh_place = jnp.sum(
        jnp.where(fresh_of[None, :] == number[:, None], code[None, :], 0), axis=1
    )
    return tags, take, fresh_place


def on_device(
    hidden_in,
    attn_gain,
    q_weight,
    key_weight_matrix,
    value_weight_matrix,
    o_weight,
    kv_pool,
    block_table,
    request_len,
    prefix_len,
    new_len,
    page_owner,
):
    n_section, n_tp, n_dec = (lax.axis_size(a) for a in ("section", "tp", "dec"))
    devices = n_section * n_tp * n_dec
    x = hidden_in[0]
    tokens = ROWS * n_tp
    normed = normalize(x, attn_gain)

    near_z = send(normed, 0, 1)
    far = send(normed, 2, 0)
    right = send(normed, 3, 0)
    left = send(normed, 1, 0)
    right_z = send(near_z, 3, 0)
    left_z = send(near_z, 1, 0)
    far_z = send(far, 0, 1)
    gathered = (normed, near_z, right, left, right_z, left_z, far, far_z)

    tp = lax.axis_index("tp")
    px, pz = tp // 2, tp % 2
    order = jnp.stack([((px + dx) % (n_tp // 2)) * 2 + (pz ^ dz) for dx, dz in PIECES]).astype(
        jnp.int32
    )

    prefix, new_tokens, full_length = prefix_len[0], new_len[0], request_len[0]
    new_ends = jnp.cumsum(new_tokens).astype(jnp.int32)
    table = block_table[0, 0]
    fresh_count = tokens // PAGE_TOKENS
    cos, sin = token_tables(prefix, new_tokens, new_ends, tokens)
    tags, take, fresh_place = page_plan(
        prefix, new_tokens, new_ends, full_length, table, page_owner[0, :, 0], devices, fresh_count
    )
    pool = kv_pool[0, :, :, 0, :]
    buffer, prefix_pages = build_pages(take, table, pool)

    by_tp = lax.dynamic_index_in_dim(
        tags.reshape(n_section, n_tp, n_dec, CAP), tp, axis=1, keepdims=False
    ).reshape(n_section * n_dec, CAP)
    own_tags = lax.all_to_all(by_tp, ("section", "dec"), split_axis=0, concat_axis=0, tiled=True)
    received_tags = jnp.broadcast_to(
        own_tags.reshape(n_section, 1, n_dec, CAP), (n_section, n_tp, n_dec, CAP)
    ).reshape(1, devices, CAP)

    q, kv = project(
        order, gathered, q_weight[0], key_weight_matrix[0], value_weight_matrix[0], cos, sin
    )
    buffer = patch_pages(
        fresh_place, kv.reshape(fresh_count, PAGE_TOKENS, 2 * HEAD_DIMENSION), buffer
    )
    received_pages = lax.all_to_all(
        buffer.reshape(devices, CAP, PAGE_TOKENS, 2 * HEAD_DIMENSION),
        ("section", "tp", "dec"),
        split_axis=0,
        concat_axis=0,
        tiled=True,
    )

    attended = attend(
        order, new_ends, prefix, q, kv, prefix_pages.reshape(-1, 2 * HEAD_DIMENSION)
    )
    parts = dict(zip(PIECES, out_project(attended, o_weight[0])))

    def total(*terms):
        return sum(t.astype(jnp.float32) for t in terms)

    far_pair = send(parts[2, 1], 0, 1)
    from_left_z = send(parts[1, 1], 1, 0)
    from_right_z = send(parts[3, 1], 3, 0)
    from_left = send(parts[1, 0], 1, 0)
    from_right = send(parts[3, 0], 3, 0)
    from_far = send(total(parts[2, 0], far_pair).astype(jnp.bfloat16), 2, 0)
    from_z = send(
        total(parts[0, 1], from_left_z, from_right_z).astype(jnp.bfloat16), 0, 1
    )
    mixed = total(x, parts[0, 0], from_left, from_right, from_z, from_far).astype(jnp.bfloat16)
    passed = shifted(mixed, "section", 1)[None]
    return passed, received_pages[None, :, :, :, None, :], received_tags


def solution(mesh):
    in_specs = (
        P("section", ("dec", "tp"), None),
        P("section", None),
        P("section", None, "tp"),
        P("section", None, "tp"),
        P("section", None, "tp"),
        P("section", "tp", None),
        P("section", "dec", None, "tp", None),
        P("section", "dec", None),
        P("section", "dec"),
        P("section", "dec"),
        P("section", "dec"),
        P("section", "dec", None),
    )
    out_specs = (
        P("section", ("dec", "tp"), None),
        P(("section", "tp", "dec"), None, None, None, None, None),
        P(("section", "tp", "dec"), None, None),
    )
    return jax.shard_map(
        on_device, mesh=mesh, in_specs=in_specs, out_specs=out_specs, check_vma=False
    )
```

```python
import functools
import math

import jax
import jax.numpy as jnp
from jax import lax
from jax.experimental import pallas as pl
from jax.experimental.pallas import tpu as pltpu
from jax.sharding import PartitionSpec as P

HEAD_DIMENSION = 128
PAGE_TOKENS = 16
MAXB = 40
NB = 56
CAP = 3
EARLY = 2
ROWS = 32

theta_base = 500000.0
eps_norm = 1e-05
neg_large = -1e30

MIB = 1 << 20
VMEM = pl.BlockSpec(memory_space=pltpu.VMEM)
SMEM = pl.BlockSpec(memory_space=pltpu.SMEM)
ANY = pl.BlockSpec(memory_space=pl.ANY)

PIECES = ((0, 0), (0, 1), (1, 0), (3, 0), (1, 1), (3, 1), (2, 0), (2, 1))


def tp_route(dx, dz, n_tp):
    nx = n_tp // 2
    return [(x * 2 + z, ((x + dx) % nx) * 2 + (z ^ dz)) for x in range(nx) for z in range(2)]


def send(block, dx, dz):
    return lax.ppermute(block, "tp", tp_route(dx, dz, lax.axis_size("tp")))


def shifted(block, axis, distance):
    count = lax.axis_size(axis)
    return lax.ppermute(block, axis, [((i - distance) % count, i) for i in range(count)])


def send_on(block, dx, dz):
    n_section, n_tp = lax.axis_size("section"), lax.axis_size("tp")
    pairs = [
        (s * n_tp + a, ((s + 1) % n_section) * n_tp + b)
        for s in range(n_section)
        for a, b in tp_route(dx, dz, n_tp)
    ]
    return lax.ppermute(block, ("section", "tp"), pairs)


def norm_kernel(x_ref, gain_ref, out_ref, x_s, gain_s, sems):
    copies = (
        pltpu.make_async_copy(x_ref, x_s, sems.at[0]),
        pltpu.make_async_copy(gain_ref, gain_s, sems.at[1]),
    )
    for copy in copies:
        copy.start()
    for copy in copies:
        copy.wait()
    x = x_s[...].astype(jnp.float32)
    scale = lax.rsqrt(jnp.mean(x * x, axis=-1, keepdims=True) + eps_norm)
    out_ref[...] = (x * scale * gain_s[...]).astype(jnp.bfloat16)


def in_hbm(array):
    return pltpu.with_memory_space_constraint(array, pltpu.HBM)


def in_vmem(array):
    return pltpu.with_memory_space_constraint(array, pltpu.VMEM)


def normalize(x, gain):
    return pl.pallas_call(
        norm_kernel,
        out_shape=jax.ShapeDtypeStruct(x.shape, jnp.bfloat16),
        in_specs=[ANY, ANY],
        out_specs=VMEM,
        scratch_shapes=[
            pltpu.VMEM(x.shape, x.dtype),
            pltpu.VMEM(gain.shape, gain.dtype),
            pltpu.SemaphoreType.DMA((2,)),
        ],
        compiler_params=pltpu.CompilerParams(vmem_limit_bytes=16 * MIB),
        cost_estimate=pl.CostEstimate(flops=4 * x.size, bytes_accessed=4 * x.size, transcendentals=0),
        name="norm",
    )(in_hbm(x), in_hbm(gain))


def project_rows(pieces, w_ref, acc_ref):
    depth = w_ref.shape[0]
    block = 2048
    for c in range(depth // block):
        cols = slice(c * block, (c + 1) * block)
        x = jnp.concatenate([p[:, cols] for p in pieces], axis=0)
        part = jnp.dot(x, w_ref[cols, :], preferred_element_type=jnp.float32)
        acc_ref[...] = part if c == 0 else acc_ref[...] + part


def rotate(v, cos, sin):
    return v * cos + pltpu.roll(v, HEAD_DIMENSION // 2, 1) * sin


def qkv_kernel(order, place, *refs):
    pieces = refs[:8]
    wq, wkv, cos_ref, sin_ref = refs[8:12]
    q_ref, kv_ref, early_ref, late_ref, acc_q, acc_kv, sems = refs[14:]
    slots = late_ref.shape[0] * CAP
    count = kv_ref.shape[0] // PAGE_TOKENS
    heads = acc_q.shape[1] // HEAD_DIMENSION

    project_rows(pieces, wkv, acc_kv)
    for p in range(8):
        rows = pl.ds(pl.multiple_of(order[p] * ROWS, ROWS), ROWS)
        here = slice(p * ROWS, (p + 1) * ROWS)
        kv_ref[rows, :HEAD_DIMENSION] = rotate(
            acc_kv[here, :HEAD_DIMENSION], cos_ref[rows, :], sin_ref[rows, :]
        ).astype(jnp.bfloat16)
        kv_ref[rows, HEAD_DIMENSION:] = acc_kv[here, HEAD_DIMENSION:].astype(jnp.bfloat16)

    def each(i, act):
        at = jnp.minimum(place[0, i], slots - 1)
        owner, slot = at // CAP, at % CAP
        page = kv_ref.at[pl.ds(i * PAGE_TOKENS, PAGE_TOKENS), :]

        @pl.when((place[0, i] < slots) & (slot < EARLY))
        def _():
            to = early_ref.at[owner * EARLY + jnp.minimum(slot, EARLY - 1)]
            act(pltpu.make_async_copy(page, to, sems.at[i]))

        @pl.when((place[0, i] < slots) & (slot >= EARLY))
        def _():
            act(pltpu.make_async_copy(page, late_ref.at[owner], sems.at[i]))

    for i in range(count):
        each(i, lambda copy: copy.start())

    project_rows(pieces, wq, acc_q)
    for p in range(8):
        rows = pl.ds(pl.multiple_of(order[p] * ROWS, ROWS), ROWS)
        here = slice(p * ROWS, (p + 1) * ROWS)
        for h in range(heads):
            cols = slice(h * HEAD_DIMENSION, (h + 1) * HEAD_DIMENSION)
            q_ref[rows, cols] = rotate(
                acc_q[here, cols], cos_ref[rows, :], sin_ref[rows, :]
            ).astype(jnp.bfloat16)

    for i in range(count):
        each(i, lambda copy: copy.wait())


def project(order, place, pieces, wq, wkv, cos, sin, early, late):
    depth, n_q = wq.shape
    n_kv = wkv.shape[1]
    tokens = 8 * ROWS
    return pl.pallas_call(
        qkv_kernel,
        in_specs=[SMEM, SMEM] + [VMEM] * 12 + [ANY, ANY],
        out_specs=[VMEM, VMEM, ANY, ANY],
        out_shape=[
            jax.ShapeDtypeStruct((tokens, n_q), jnp.bfloat16),
            jax.ShapeDtypeStruct((tokens, n_kv), jnp.bfloat16),
            pltpu.HBM(early.shape, early.dtype),
            pltpu.HBM(late.shape, late.dtype),
        ],
        scratch_shapes=[
            pltpu.VMEM((tokens, n_q), jnp.float32),
            pltpu.VMEM((tokens, n_kv), jnp.float32),
            pltpu.SemaphoreType.DMA((tokens // PAGE_TOKENS,)),
        ],
        input_output_aliases={14: 2, 15: 3},
        compiler_params=pltpu.CompilerParams(vmem_limit_bytes=12 * MIB),
        cost_estimate=pl.CostEstimate(
            flops=2 * tokens * depth * (n_q + n_kv),
            bytes_accessed=2 * depth * (n_q + n_kv + tokens),
            transcendentals=0,
        ),
        name="qkv",
    )(order, place, *pieces, in_vmem(wq), in_vmem(wkv), cos, sin, early, late)


def prepare_kernel(
    devices,
    prefix_len_in,
    new_len_in,
    full_len_in,
    table_in,
    owner_in,
    pool_in,
    frequency_ref,
    wq_ref,
    wk_ref,
    wv_ref,
    angles_ref,
    early_ref,
    late_ref,
    prefix_ref,
    place_ref,
    wq_out,
    wkv_out,
    prefix_len_ref,
    new_len_ref,
    full_len_ref,
    table_ref,
    owner_ref,
    pool_ref,
    take_v,
    take_s,
    sems,
):
    pairs = (
        (prefix_len_in, prefix_len_ref),
        (new_len_in, new_len_ref),
        (full_len_in, full_len_ref),
        (table_in, table_ref),
        (owner_in, owner_ref),
        (pool_in, pool_ref),
        (wk_ref, wkv_out.at[:, pl.ds(0, HEAD_DIMENSION)]),
        (wv_ref, wkv_out.at[:, pl.ds(HEAD_DIMENSION, HEAD_DIMENSION)]),
        (wq_ref, wq_out),
    )
    copies = [pltpu.make_async_copy(a, b, sems.at[i]) for i, (a, b) in enumerate(pairs)]
    for copy in copies:
        copy.start()
    for copy in copies[:5]:
        copy.wait()

    requests = prefix_len_ref.shape[1]
    rows = owner_ref.shape[1]
    old = [prefix_len_ref[0, r] // PAGE_TOKENS for r in range(requests)]
    new = [new_len_ref[0, r] // PAGE_TOKENS for r in range(requests)]
    open_ = [
        full_len_ref[0, r] != prefix_len_ref[0, r] + new_len_ref[0, r] for r in range(requests)
    ]
    base = [0]
    for r in range(requests - 1):
        base.append(base[r] + new[r])

    def by_request(row, values):
        out = jnp.full(row.shape, values[0], jnp.int32)
        for r in range(1, requests):
            out = jnp.where(row >= r * NB, values[r], out)
        return out

    def targets(row, owner):
        block = row - by_request(row, [r * NB for r in range(requests)])
        kept = by_request(row, [jnp.where(open_[r], 0, old[r] + new[r]) for r in range(requests)])
        return block, jnp.where(block < kept, owner, devices)

    row = lax.broadcasted_iota(jnp.int32, (rows, 1), 0)
    lane = lax.broadcasted_iota(jnp.int32, (1, rows), 1)
    owner = owner_ref[...]
    block, target = targets(
        row, jnp.sum(jnp.where(lane == row, owner, 0), axis=1, keepdims=True)
    )
    _, across = targets(lane, owner)
    rank = jnp.sum(
        jnp.where((across == target) & (lane < row), 1, 0), axis=1, keepdims=True
    )
    slots = devices * CAP
    code = jnp.where(target < devices, target * CAP + rank, slots)
    ages = by_request(row, old)
    first = by_request(row, [r * MAXB for r in range(requests)])
    source = jnp.where(block < ages, first + block + 1, 0)
    hit = code == lax.broadcasted_iota(jnp.int32, (1, slots), 1)
    take_v[...] = jnp.sum(jnp.where(hit, source, 0), axis=0, keepdims=True) - 1
    taken = pltpu.make_async_copy(take_v, take_s, sems.at[len(pairs)])
    taken.start()
    fresh = jnp.where(
        (block >= ages) & (block < by_request(row, [old[r] + new[r] for r in range(requests)])),
        by_request(row, base) + block - ages,
        -1,
    )
    number = lax.broadcasted_iota(jnp.int32, place_ref.shape, 1)
    place_ref[...] = jnp.sum(jnp.where(fresh == number, code, 0), axis=0, keepdims=True)

    token = lax.broadcasted_iota(jnp.int32, (angles_ref.shape[0], 1), 0)
    shift = jnp.full(token.shape, prefix_len_ref[0, 0], jnp.int32)
    for r in range(1, requests):
        start = base[r] * PAGE_TOKENS
        shift = jnp.where(token >= start, prefix_len_ref[0, r] - start, shift)
    angles_ref[...] = (token + shift).astype(jnp.float32) * frequency_ref[...]

    copies[5].wait()

    def gather(i, _):
        prefix_ref[i] = pool_ref[table_ref[0, i]]
        return 0

    lax.fori_loop(0, prefix_ref.shape[0], gather, 0, unroll=8)
    taken.wait()

    def page(i):
        at = take_s[0, i]
        found = pool_ref[table_ref[0, jnp.maximum(at, 0)]]
        return jnp.where(at >= 0, found, jnp.zeros_like(found))

    def fill(o, _):
        for j in range(EARLY):
            early_ref[o * EARLY + j] = page(o * CAP + j)
        late_ref[o] = page(o * CAP + EARLY)
        return 0

    lax.fori_loop(0, devices, fill, 0, unroll=4)
    for copy in copies[6:]:
        copy.wait()


def prepare(
    devices, tokens, prefix_len, new_len, full_len, table, owner, pool, wq, wk, wv
):
    slots = devices * CAP
    half = HEAD_DIMENSION // 2
    frequency = theta_base ** (-(jnp.arange(half, dtype=jnp.float32) * 2.0) / HEAD_DIMENSION)
    depth = wq.shape[0]
    return pl.pallas_call(
        functools.partial(prepare_kernel, devices),
        out_shape=[
            jax.ShapeDtypeStruct((tokens, half), jnp.float32),
            pltpu.HBM((devices * EARLY,) + pool.shape[1:], pool.dtype),
            pltpu.HBM((devices,) + pool.shape[1:], pool.dtype),
            jax.ShapeDtypeStruct((table.shape[1],) + pool.shape[1:], pool.dtype),
            jax.ShapeDtypeStruct((1, 128), jnp.int32),
            pltpu.VMEM(wq.shape, wq.dtype),
            pltpu.VMEM((depth, 2 * HEAD_DIMENSION), wk.dtype),
        ],
        in_specs=[ANY] * 6 + [VMEM] + [ANY] * 3,
        out_specs=[VMEM] * 7,
        scratch_shapes=[
            pltpu.SMEM(prefix_len.shape, jnp.int32),
            pltpu.SMEM(new_len.shape, jnp.int32),
            pltpu.SMEM(full_len.shape, jnp.int32),
            pltpu.SMEM(table.shape, jnp.int32),
            pltpu.VMEM(owner.shape, jnp.int32),
            pltpu.VMEM(pool.shape, pool.dtype),
            pltpu.VMEM((1, slots), jnp.int32),
            pltpu.SMEM((1, slots), jnp.int32),
            pltpu.SemaphoreType.DMA((10,)),
        ],
        compiler_params=pltpu.CompilerParams(vmem_limit_bytes=16 * MIB),
        cost_estimate=pl.CostEstimate(flops=0, bytes_accessed=20 * MIB, transcendentals=0),
        name="prepare",
    )(
        in_hbm(prefix_len),
        in_hbm(new_len),
        in_hbm(full_len),
        in_hbm(table),
        in_hbm(owner),
        in_hbm(pool),
        frequency[None, :],
        in_hbm(wq),
        in_hbm(wk),
        in_hbm(wv),
    )


TILE = 64


def attention_kernel(
    order_ref, new_len_ref, prefix_len_ref, q_ref, kv_ref, prefix_in, w_ref, *rest
):
    outs, (prefix_ref, x_ref, q_s, o_s, w_s, y_s, sems, out_sems, prefix_sem) = rest[:8], rest[8:]
    prefix_copy = pltpu.make_async_copy(prefix_in, prefix_ref, prefix_sem)
    prefix_copy.start()
    chunk = w_s.shape[2]

    def weights(c):
        return pltpu.make_async_copy(w_ref.at[:, pl.ds(c * chunk, chunk)], w_s.at[c], sems.at[c])

    def written(c, p):
        return pltpu.make_async_copy(
            y_s.at[c, pl.ds(p * ROWS, ROWS), :],
            outs[p].at[:, pl.ds(c * chunk, chunk)],
            out_sems.at[c, p],
        )


    tokens = q_ref.shape[0]
    heads = q_ref.shape[1] // HEAD_DIMENSION
    tiles = tokens // TILE
    requests = new_len_ref.shape[1]
    slots = MAXB * PAGE_TOKENS
    for j in range(tiles):
        for h in range(heads):
            q_s[j, h * TILE : (h + 1) * TILE, :] = q_ref[
                j * TILE : (j + 1) * TILE, h * HEAD_DIMENSION : (h + 1) * HEAD_DIMENSION
            ]
    prefix_copy.wait()
    for c in range(w_s.shape[0]):
        weights(c).start()
    scale = 1.0 / math.sqrt(HEAD_DIMENSION)
    nt = (((1,), (1,)), ((), ()))

    def body(i, _):
        j, r = i // requests, i % requests
        start = 0
        for i in range(requests - 1):
            start = start + jnp.where(i < r, new_len_ref[0, i], 0)
        end = start + new_len_ref[0, r]

        @pl.when((start < (j + 1) * TILE) & (end > j * TILE))
        def _():
            q = q_s[j]
            rows = pl.ds(pl.multiple_of(r * slots, slots), slots)
            s1 = lax.dot_general(
                q, prefix_ref[rows, :HEAD_DIMENSION], nt, preferred_element_type=jnp.float32
            )
            s2 = lax.dot_general(
                q, kv_ref[:, :HEAD_DIMENSION], nt, preferred_element_type=jnp.float32
            )
            slot = lax.broadcasted_iota(jnp.int32, s1.shape, 1)
            s1 = jnp.where(slot < prefix_len_ref[0, r], s1 * scale, neg_large)
            token = j * TILE + lax.rem(lax.broadcasted_iota(jnp.int32, s2.shape, 0), TILE)
            key = lax.broadcasted_iota(jnp.int32, s2.shape, 1)
            s2 = jnp.where((key >= start) & (key <= token), s2 * scale, neg_large)
            top = jnp.maximum(
                jnp.max(s1, axis=1, keepdims=True), jnp.max(s2, axis=1, keepdims=True)
            )
            p1 = jnp.exp(s1 - top)
            p2 = jnp.exp(s2 - top)
            total = jnp.sum(p1, axis=1, keepdims=True) + jnp.sum(p2, axis=1, keepdims=True)
            inverse = 1.0 / total
            o = jnp.dot(
                (p1 * inverse).astype(jnp.bfloat16),
                prefix_ref[rows, HEAD_DIMENSION:],
                preferred_element_type=jnp.float32,
            ) + jnp.dot(
                (p2 * inverse).astype(jnp.bfloat16),
                kv_ref[:, HEAD_DIMENSION:],
                preferred_element_type=jnp.float32,
            )
            own = j * TILE + lax.rem(lax.broadcasted_iota(jnp.int32, o.shape, 0), TILE)
            mine = (own >= start) & (own < end)
            o_s[j] = jnp.where(mine, o, o_s[j])

        return 0

    lax.fori_loop(0, tiles * requests, body, 0)
    per_tile = TILE // ROWS
    for p in range(8):
        at = order_ref[p]
        tile, part = at // per_tile, at % per_tile
        for h in range(heads):
            x_ref[p * ROWS : (p + 1) * ROWS, h * HEAD_DIMENSION : (h + 1) * HEAD_DIMENSION] = o_s[
                tile, pl.ds(pl.multiple_of(h * TILE + part * ROWS, ROWS), ROWS), :
            ].astype(jnp.bfloat16)
    for c in range(w_s.shape[0]):
        weights(c).wait()
        y_s[c] = jnp.dot(x_ref[...], w_s[c], preferred_element_type=jnp.float32).astype(
            jnp.bfloat16
        )
        for p in range(8):
            written(c, p).start()
    for c in range(w_s.shape[0]):
        for p in range(8):
            written(c, p).wait()


def attend(order, new_len, prefix_len, q, kv, prefix, w):
    tokens, width = q.shape
    heads = width // HEAD_DIMENSION
    columns = w.shape[1]
    chunk = 2048
    work = 2 * tokens * heads * (MAXB * PAGE_TOKENS + tokens) * HEAD_DIMENSION * 2 * 2
    return pl.pallas_call(
        attention_kernel,
        out_shape=[pltpu.HBM((ROWS, columns), jnp.bfloat16)] * 8,
        in_specs=[SMEM, SMEM, SMEM, VMEM, VMEM, ANY, ANY],
        out_specs=[ANY] * 8,
        scratch_shapes=[
            pltpu.VMEM(prefix.shape, prefix.dtype),
            pltpu.VMEM((tokens, width), jnp.bfloat16),
            pltpu.VMEM((tokens // TILE, heads * TILE, HEAD_DIMENSION), jnp.bfloat16),
            pltpu.VMEM((tokens // TILE, heads * TILE, HEAD_DIMENSION), jnp.float32),
            pltpu.VMEM((columns // chunk, width, chunk), jnp.bfloat16),
            pltpu.VMEM((columns // chunk, tokens, chunk), jnp.bfloat16),
            pltpu.SemaphoreType.DMA((columns // chunk,)),
            pltpu.SemaphoreType.DMA((columns // chunk, 8)),
            pltpu.SemaphoreType.DMA,
        ],
        compiler_params=pltpu.CompilerParams(vmem_limit_bytes=28 * MIB),
        cost_estimate=pl.CostEstimate(
            flops=0, bytes_accessed=0, transcendentals=0
        ),
        name="attention",
    )(order, new_len, prefix_len, q, kv, in_hbm(prefix), in_hbm(w))


def merge_kernel(early_ref, late_ref, out_ref):
    out_ref[:, :EARLY] = early_ref[...]
    out_ref[:, EARLY:] = late_ref[...]


def merged(early, late):
    devices = early.shape[0]
    page = early.shape[2:]

    def spec(slots):
        return pl.BlockSpec((devices // 8, slots) + page, lambda i: (i, 0, 0, 0))

    return pl.pallas_call(
        merge_kernel,
        grid=(8,),
        in_specs=[spec(EARLY), spec(CAP - EARLY)],
        out_specs=spec(CAP),
        out_shape=jax.ShapeDtypeStruct((devices, CAP) + page, early.dtype),
        compiler_params=pltpu.CompilerParams(vmem_limit_bytes=16 * MIB),
        cost_estimate=pl.CostEstimate(flops=0, bytes_accessed=6 * MIB, transcendentals=0),
        name="keep",
    )(early, late)


def rotary_tables(angles):
    cosine, sine = jnp.cos(angles), jnp.sin(angles)
    return (
        jnp.concatenate([cosine, cosine], axis=1),
        jnp.concatenate([-sine, sine], axis=1),
    )


def page_tags(groups, me, requests):
    rows = requests * NB
    owners = groups[:, :rows]
    prefix, new_tokens, full_length = (
        groups[:, rows + i * requests : rows + (i + 1) * requests] for i in range(3)
    )
    block = jnp.arange(NB, dtype=jnp.int32)
    pages = jnp.where(
        full_length == prefix + new_tokens, (prefix + new_tokens) // PAGE_TOKENS, 0
    )
    sent = (block < pages[:, :, None]).reshape(-1, rows)
    number = jnp.where((owners == me) & sent, jnp.arange(1, rows + 1, dtype=jnp.int32), rows + 1)
    tags = []
    last = jnp.zeros((groups.shape[0], 1), jnp.int32)
    for _ in range(CAP):
        last = jnp.min(jnp.where(number > last, number, rows + 1), axis=1, keepdims=True)
        tags.append(jnp.where(last <= rows, last, 0))
    return jnp.concatenate(tags, axis=1)


def on_device(
    hidden_in,
    attn_gain,
    q_weight,
    key_weight_matrix,
    value_weight_matrix,
    o_weight,
    kv_pool,
    block_table,
    request_len,
    prefix_len,
    new_len,
    page_owner,
):
    n_section, n_tp, n_dec = (lax.axis_size(a) for a in ("section", "tp", "dec"))
    devices = n_section * n_tp * n_dec
    x = hidden_in[0]
    tokens = ROWS * n_tp
    normed = normalize(x, attn_gain)

    far = send(normed, 2, 0)
    near_z = send(normed, 0, 1)
    right = send(normed, 3, 0)
    left = send(normed, 1, 0)

    tp = lax.axis_index("tp")
    px, pz = tp // 2, tp % 2
    order = jnp.stack([((px + dx) % (n_tp // 2)) * 2 + (pz ^ dz) for dx, dz in PIECES]).astype(
        jnp.int32
    )

    prefix, new_tokens, full_length = prefix_len[0], new_len[0], request_len[0]
    owners = page_owner[0, :, 0]
    plain = jnp.concatenate([owners, prefix, new_tokens, full_length])
    near_z, owner_row = lax.optimization_barrier((near_z, owners[None, :]))
    right_z = send(near_z, 3, 0)
    left_z = send(near_z, 1, 0)
    plain, normed = lax.optimization_barrier((plain, normed))
    groups = lax.all_to_all(
        jnp.broadcast_to(plain, (n_section * n_dec,) + plain.shape),
        ("section", "dec"),
        split_axis=0,
        concat_axis=0,
        tiled=True,
    )
    groups, far = lax.optimization_barrier((groups, far))
    far_z = send(far, 0, 1)
    gathered = (normed, near_z, right, left, right_z, left_z, far, far_z)

    pool = kv_pool[0, :, :, 0, :]
    angles, early, late, prefix_pages, place, wq, wkv = prepare(
        devices,
        tokens,
        prefix_len,
        new_len,
        request_len,
        block_table[0],
        owner_row,
        pool,
        q_weight[0],
        key_weight_matrix[0],
        value_weight_matrix[0],
    )
    cos, sin = rotary_tables(angles)
    q, kv, early, late = project(order, place, gathered, wq, wkv, cos, sin, early, late)

    def deliver(pages):
        return lax.all_to_all(
            pages.reshape(devices, -1, PAGE_TOKENS, 2 * HEAD_DIMENSION),
            ("section", "tp", "dec"),
            split_axis=0,
            concat_axis=0,
            tiled=True,
        )

    early = deliver(early)
    parts = dict(
        zip(
            PIECES,
            attend(
                order,
                new_len,
                prefix_len,
                q,
                kv,
                prefix_pages.reshape(-1, 2 * HEAD_DIMENSION),
                o_weight[0],
            ),
        )
    )

    far_pair = send(parts[2, 1], 0, 1)
    from_left_z = send(parts[1, 1], 1, 0)
    from_right_z = send(parts[3, 1], 3, 0)

    early, far_pair, from_left_z, from_right_z = lax.optimization_barrier(
        (early, far_pair, from_left_z, from_right_z)
    )

    def total(*terms):
        return sum(t.astype(jnp.float32) for t in terms)

    from_left = send(parts[1, 0], 1, 0)
    from_right = send(parts[3, 0], 3, 0)
    from_far = send(total(parts[2, 0], far_pair).astype(jnp.bfloat16), 2, 0)
    from_z = send_on(total(parts[0, 1], from_left_z, from_right_z).astype(jnp.bfloat16), 0, 1)
    own = send_on(
        total(x, parts[0, 0], from_left, from_right, from_far).astype(jnp.bfloat16), 0, 0
    )
    kept = merged(early, deliver(late))
    passed = total(own, from_z).astype(jnp.bfloat16)[None]

    me = (lax.axis_index("section") * n_tp + tp) * n_dec + lax.axis_index("dec")
    received_tags = jnp.broadcast_to(
        page_tags(groups, me, prefix.shape[0]).reshape(n_section, 1, n_dec, CAP),
        (n_section, n_tp, n_dec, CAP),
    ).reshape(1, devices, CAP)
    return passed, kept[None, :, :, :, None, :], received_tags


def solution(mesh):
    in_specs = (
        P("section", ("dec", "tp"), None),
        P("section", None),
        P("section", None, "tp"),
        P("section", None, "tp"),
        P("section", None, "tp"),
        P("section", "tp", None),
        P("section", "dec", None, "tp", None),
        P("section", "dec", None),
        P("section", "dec"),
        P("section", "dec"),
        P("section", "dec"),
        P("section", "dec", None),
    )
    out_specs = (
        P("section", ("dec", "tp"), None),
        P(("section", "tp", "dec"), None, None, None, None, None),
        P(("section", "tp", "dec"), None, None),
    )
    return jax.shard_map(
        on_device, mesh=mesh, in_specs=in_specs, out_specs=out_specs, check_vma=False
    )
```

```python
import functools
import math

import jax
import jax.numpy as jnp
from jax import lax
from jax.experimental import pallas as pl
from jax.experimental.pallas import tpu as pltpu
from jax.sharding import PartitionSpec as P

HEAD_DIMENSION = 128
PAGE_TOKENS = 16
MAXB = 40
NB = 56
CAP = 3
SOON = 5
ROWS = 32

theta_base = 500000.0
eps_norm = 1e-05
neg_large = -1e30

MIB = 1 << 20
VMEM = pl.BlockSpec(memory_space=pltpu.VMEM)
SMEM = pl.BlockSpec(memory_space=pltpu.SMEM)
ANY = pl.BlockSpec(memory_space=pl.ANY)

PIECES = ((0, 0), (0, 1), (1, 0), (3, 0), (2, 0), (1, 1), (3, 1), (2, 1))


def tp_route(dx, dz, n_tp):
    nx = n_tp // 2
    return [(x * 2 + z, ((x + dx) % nx) * 2 + (z ^ dz)) for x in range(nx) for z in range(2)]


def send(block, dx, dz):
    return lax.ppermute(block, "tp", tp_route(dx, dz, lax.axis_size("tp")))


def shifted(block, axis, distance):
    count = lax.axis_size(axis)
    return lax.ppermute(block, axis, [((i - distance) % count, i) for i in range(count)])


def norm_kernel(x_ref, gain_ref, out_ref, x_s, gain_s, sems):
    copies = (
        pltpu.make_async_copy(x_ref, x_s, sems.at[0]),
        pltpu.make_async_copy(gain_ref, gain_s, sems.at[1]),
    )
    for copy in copies:
        copy.start()
    for copy in copies:
        copy.wait()
    x = x_s[...].astype(jnp.float32)
    scale = lax.rsqrt(jnp.mean(x * x, axis=-1, keepdims=True) + eps_norm)
    out_ref[...] = (x * scale * gain_s[...]).astype(jnp.bfloat16)


def in_hbm(array):
    return pltpu.with_memory_space_constraint(array, pltpu.HBM)


def in_vmem(array):
    return pltpu.with_memory_space_constraint(array, pltpu.VMEM)


def normalize(x, gain):
    return pl.pallas_call(
        norm_kernel,
        out_shape=jax.ShapeDtypeStruct(x.shape, jnp.bfloat16),
        in_specs=[ANY, ANY],
        out_specs=VMEM,
        scratch_shapes=[
            pltpu.VMEM(x.shape, x.dtype),
            pltpu.VMEM(gain.shape, gain.dtype),
            pltpu.SemaphoreType.DMA((2,)),
        ],
        compiler_params=pltpu.CompilerParams(vmem_limit_bytes=16 * MIB),
        cost_estimate=pl.CostEstimate(flops=4 * x.size, bytes_accessed=4 * x.size, transcendentals=0),
        name="norm",
    )(in_hbm(x), in_hbm(gain))


def project_rows(pieces, w_ref, acc_ref):
    depth = w_ref.shape[0]
    block = 2048
    for c in range(depth // block):
        cols = slice(c * block, (c + 1) * block)
        x = jnp.concatenate([p[:, cols] for p in pieces], axis=0)
        part = jnp.dot(x, w_ref[cols, :], preferred_element_type=jnp.float32)
        acc_ref[...] = part if c == 0 else acc_ref[...] + part


def rotate(v, cos, sin):
    return v * cos + pltpu.roll(v, HEAD_DIMENSION // 2, 1) * sin


def write_rows(order, first, count, acc_q, acc_kv, cos_ref, sin_ref, q_ref, kv_ref):
    heads = acc_q.shape[1] // HEAD_DIMENSION
    for p in range(count):
        rows = pl.ds(pl.multiple_of(order[first + p] * ROWS, ROWS), ROWS)
        here = slice(p * ROWS, (p + 1) * ROWS)
        cos, sin = cos_ref[rows, :], sin_ref[rows, :]
        kv_ref[rows, :HEAD_DIMENSION] = rotate(acc_kv[here, :HEAD_DIMENSION], cos, sin).astype(
            jnp.bfloat16
        )
        kv_ref[rows, HEAD_DIMENSION:] = acc_kv[here, HEAD_DIMENSION:].astype(jnp.bfloat16)
        for h in range(heads):
            cols = slice(h * HEAD_DIMENSION, (h + 1) * HEAD_DIMENSION)
            q_ref[rows, cols] = rotate(acc_q[here, cols], cos, sin).astype(jnp.bfloat16)


def first_kernel(order, *refs):
    pieces = refs[:SOON]
    wq, wkv, cos_ref, sin_ref, q_ref, kv_ref, acc_q, acc_kv = refs[SOON:]
    project_rows(pieces, wkv, acc_kv)
    project_rows(pieces, wq, acc_q)
    q_ref[...] = jnp.zeros_like(q_ref)
    kv_ref[...] = jnp.zeros_like(kv_ref)
    write_rows(order, 0, SOON, acc_q, acc_kv, cos_ref, sin_ref, q_ref, kv_ref)


def project_first(order, pieces, wq, wkv, cos, sin):
    depth, n_q = wq.shape
    n_kv = wkv.shape[1]
    tokens = 8 * ROWS
    rows = SOON * ROWS
    return pl.pallas_call(
        first_kernel,
        in_specs=[SMEM] + [VMEM] * (SOON + 4),
        out_specs=[VMEM, VMEM],
        out_shape=[
            jax.ShapeDtypeStruct((tokens, n_q), jnp.bfloat16),
            jax.ShapeDtypeStruct((tokens, n_kv), jnp.bfloat16),
        ],
        scratch_shapes=[
            pltpu.VMEM((rows, n_q), jnp.float32),
            pltpu.VMEM((rows, n_kv), jnp.float32),
        ],
        compiler_params=pltpu.CompilerParams(vmem_limit_bytes=12 * MIB),
        cost_estimate=pl.CostEstimate(
            flops=2 * rows * depth * (n_q + n_kv),
            bytes_accessed=2 * depth * (n_q + n_kv + rows),
            transcendentals=0,
        ),
        name="qkv_first",
    )(order, *pieces, in_vmem(wq), in_vmem(wkv), cos, sin)


def qkv_kernel(order, place, *refs):
    pieces = refs[: 8 - SOON]
    wq, wkv, cos_ref, sin_ref, q_in, kv_in, buffer_ref = refs[8 - SOON : 15 - SOON]
    q_ref, kv_ref, out_ref, acc_q, acc_kv, sems = refs[15 - SOON :]
    del buffer_ref
    slots = out_ref.shape[0]
    count = kv_ref.shape[0] // PAGE_TOKENS
    project_rows(pieces, wkv, acc_kv)
    project_rows(pieces, wq, acc_q)
    q_ref[...] = q_in[...]
    kv_ref[...] = kv_in[...]
    write_rows(order, SOON, 8 - SOON, acc_q, acc_kv, cos_ref, sin_ref, q_ref, kv_ref)

    def copy(i):
        return pltpu.make_async_copy(
            kv_ref.at[pl.ds(i * PAGE_TOKENS, PAGE_TOKENS), :],
            out_ref.at[jnp.minimum(place[0, i], slots - 1)],
            sems.at[i],
        )

    for i in range(count):
        @pl.when(place[0, i] < slots)
        def _():
            copy(i).start()

    for i in range(count):
        @pl.when(place[0, i] < slots)
        def _():
            copy(i).wait()


def project(order, place, pieces, wq, wkv, cos, sin, buffer):
    depth, n_q = wq.shape
    n_kv = wkv.shape[1]
    tokens = 8 * ROWS
    rows = (8 - SOON) * ROWS
    q, kv = project_first(order, pieces[:SOON], wq, wkv, cos, sin)
    return pl.pallas_call(
        qkv_kernel,
        in_specs=[SMEM, SMEM] + [VMEM] * (8 - SOON + 6) + [ANY],
        out_specs=[VMEM, VMEM, ANY],
        out_shape=[
            jax.ShapeDtypeStruct((tokens, n_q), jnp.bfloat16),
            jax.ShapeDtypeStruct((tokens, n_kv), jnp.bfloat16),
            pltpu.HBM(buffer.shape, buffer.dtype),
        ],
        scratch_shapes=[
            pltpu.VMEM((rows, n_q), jnp.float32),
            pltpu.VMEM((rows, n_kv), jnp.float32),
            pltpu.SemaphoreType.DMA((tokens // PAGE_TOKENS,)),
        ],
        input_output_aliases={16 - SOON: 2},
        compiler_params=pltpu.CompilerParams(vmem_limit_bytes=12 * MIB),
        cost_estimate=pl.CostEstimate(
            flops=2 * rows * depth * (n_q + n_kv),
            bytes_accessed=2 * depth * (n_q + n_kv + rows),
            transcendentals=0,
        ),
        name="qkv",
    )(order, place, *pieces[SOON:], in_vmem(wq), in_vmem(wkv), cos, sin, q, kv, buffer)


def prepare_kernel(
    devices,
    prefix_len_in,
    new_len_in,
    full_len_in,
    table_in,
    owner_in,
    pool_in,
    frequency_ref,
    wq_ref,
    wk_ref,
    wv_ref,
    angles_ref,
    buffer_ref,
    prefix_ref,
    place_ref,
    wq_out,
    wkv_out,
    prefix_len_ref,
    new_len_ref,
    full_len_ref,
    table_ref,
    owner_ref,
    pool_ref,
    take_v,
    take_s,
    sems,
):
    pairs = (
        (prefix_len_in, prefix_len_ref),
        (new_len_in, new_len_ref),
        (full_len_in, full_len_ref),
        (table_in, table_ref),
        (owner_in, owner_ref),
        (pool_in, pool_ref),
        (wk_ref, wkv_out.at[:, pl.ds(0, HEAD_DIMENSION)]),
        (wv_ref, wkv_out.at[:, pl.ds(HEAD_DIMENSION, HEAD_DIMENSION)]),
        (wq_ref, wq_out),
    )
    copies = [pltpu.make_async_copy(a, b, sems.at[i]) for i, (a, b) in enumerate(pairs)]
    for copy in copies:
        copy.start()
    for copy in copies[:5]:
        copy.wait()

    requests = prefix_len_ref.shape[1]
    rows = owner_ref.shape[1]
    old = [prefix_len_ref[0, r] // PAGE_TOKENS for r in range(requests)]
    new = [new_len_ref[0, r] // PAGE_TOKENS for r in range(requests)]
    open_ = [
        full_len_ref[0, r] != prefix_len_ref[0, r] + new_len_ref[0, r] for r in range(requests)
    ]
    base = [0]
    for r in range(requests - 1):
        base.append(base[r] + new[r])

    def by_request(row, values):
        out = jnp.full(row.shape, values[0], jnp.int32)
        for r in range(1, requests):
            out = jnp.where(row >= r * NB, values[r], out)
        return out

    def targets(row, owner):
        block = row - by_request(row, [r * NB for r in range(requests)])
        kept = by_request(row, [jnp.where(open_[r], 0, old[r] + new[r]) for r in range(requests)])
        return block, jnp.where(block < kept, owner, devices)

    row = lax.broadcasted_iota(jnp.int32, (rows, 1), 0)
    lane = lax.broadcasted_iota(jnp.int32, (1, rows), 1)
    owner = owner_ref[...]
    block, target = targets(
        row, jnp.sum(jnp.where(lane == row, owner, 0), axis=1, keepdims=True)
    )
    _, across = targets(lane, owner)
    rank = jnp.sum(
        jnp.where((across == target) & (lane < row), 1, 0), axis=1, keepdims=True
    )
    slots = buffer_ref.shape[0]
    code = jnp.where(target < devices, target * CAP + rank, slots)
    ages = by_request(row, old)
    first = by_request(row, [r * MAXB for r in range(requests)])
    source = jnp.where(block < ages, first + block + 1, 0)
    hit = code == lax.broadcasted_iota(jnp.int32, (1, slots), 1)
    take_v[...] = jnp.sum(jnp.where(hit, source, 0), axis=0, keepdims=True) - 1
    taken = pltpu.make_async_copy(take_v, take_s, sems.at[len(pairs)])
    taken.start()
    fresh = jnp.where(
        (block >= ages) & (block < by_request(row, [old[r] + new[r] for r in range(requests)])),
        by_request(row, base) + block - ages,
        -1,
    )
    number = lax.broadcasted_iota(jnp.int32, place_ref.shape, 1)
    place_ref[...] = jnp.sum(jnp.where(fresh == number, code, 0), axis=0, keepdims=True)

    token = lax.broadcasted_iota(jnp.int32, (angles_ref.shape[0], 1), 0)
    shift = jnp.full(token.shape, prefix_len_ref[0, 0], jnp.int32)
    for r in range(1, requests):
        start = base[r] * PAGE_TOKENS
        shift = jnp.where(token >= start, prefix_len_ref[0, r] - start, shift)
    angles_ref[...] = (token + shift).astype(jnp.float32) * frequency_ref[...]

    copies[5].wait()

    def gather(i, _):
        prefix_ref[i] = pool_ref[table_ref[0, i]]
        return 0

    lax.fori_loop(0, prefix_ref.shape[0], gather, 0, unroll=8)
    taken.wait()

    def fill(i, _):
        at = take_s[0, i]
        page = pool_ref[table_ref[0, jnp.maximum(at, 0)]]
        buffer_ref[i] = jnp.where(at >= 0, page, jnp.zeros_like(page))
        return 0

    lax.fori_loop(0, slots, fill, 0, unroll=8)
    for copy in copies[6:]:
        copy.wait()


def prepare(
    devices, tokens, prefix_len, new_len, full_len, table, owner, pool, wq, wk, wv
):
    slots = devices * CAP
    half = HEAD_DIMENSION // 2
    frequency = theta_base ** (-(jnp.arange(half, dtype=jnp.float32) * 2.0) / HEAD_DIMENSION)
    depth = wq.shape[0]
    return pl.pallas_call(
        functools.partial(prepare_kernel, devices),
        out_shape=[
            jax.ShapeDtypeStruct((tokens, half), jnp.float32),
            pltpu.HBM((slots,) + pool.shape[1:], pool.dtype),
            jax.ShapeDtypeStruct((table.shape[1],) + pool.shape[1:], pool.dtype),
            jax.ShapeDtypeStruct((1, 128), jnp.int32),
            pltpu.VMEM(wq.shape, wq.dtype),
            pltpu.VMEM((depth, 2 * HEAD_DIMENSION), wk.dtype),
        ],
        in_specs=[ANY] * 6 + [VMEM] + [ANY] * 3,
        out_specs=[VMEM] * 6,
        scratch_shapes=[
            pltpu.SMEM(prefix_len.shape, jnp.int32),
            pltpu.SMEM(new_len.shape, jnp.int32),
            pltpu.SMEM(full_len.shape, jnp.int32),
            pltpu.SMEM(table.shape, jnp.int32),
            pltpu.VMEM(owner.shape, jnp.int32),
            pltpu.VMEM(pool.shape, pool.dtype),
            pltpu.VMEM((1, slots), jnp.int32),
            pltpu.SMEM((1, slots), jnp.int32),
            pltpu.SemaphoreType.DMA((10,)),
        ],
        compiler_params=pltpu.CompilerParams(vmem_limit_bytes=16 * MIB),
        cost_estimate=pl.CostEstimate(flops=0, bytes_accessed=20 * MIB, transcendentals=0),
        name="prepare",
    )(
        in_hbm(prefix_len),
        in_hbm(new_len),
        in_hbm(full_len),
        in_hbm(table),
        in_hbm(owner),
        in_hbm(pool),
        frequency[None, :],
        in_hbm(wq),
        in_hbm(wk),
        in_hbm(wv),
    )


TILE = 64


def attention_kernel(
    order_ref, new_len_ref, prefix_len_ref, q_ref, kv_ref, prefix_in, w_ref, *rest
):
    outs, (prefix_ref, x_ref, q_s, o_s, w_s, y_s, sems, out_sems, prefix_sem) = rest[:8], rest[8:]
    prefix_copy = pltpu.make_async_copy(prefix_in, prefix_ref, prefix_sem)
    prefix_copy.start()
    chunk = w_s.shape[2]

    def weights(c):
        return pltpu.make_async_copy(w_ref.at[:, pl.ds(c * chunk, chunk)], w_s.at[c], sems.at[c])

    def written(c, p):
        return pltpu.make_async_copy(
            y_s.at[c, pl.ds(p * ROWS, ROWS), :],
            outs[p].at[:, pl.ds(c * chunk, chunk)],
            out_sems.at[c, p],
        )


    tokens = q_ref.shape[0]
    heads = q_ref.shape[1] // HEAD_DIMENSION
    tiles = tokens // TILE
    requests = new_len_ref.shape[1]
    slots = MAXB * PAGE_TOKENS
    for j in range(tiles):
        for h in range(heads):
            q_s[j, h * TILE : (h + 1) * TILE, :] = q_ref[
                j * TILE : (j + 1) * TILE, h * HEAD_DIMENSION : (h + 1) * HEAD_DIMENSION
            ]
    prefix_copy.wait()
    for c in range(w_s.shape[0]):
        weights(c).start()
    scale = 1.0 / math.sqrt(HEAD_DIMENSION)
    nt = (((1,), (1,)), ((), ()))

    def body(i, _):
        j, r = i // requests, i % requests
        start = 0
        for i in range(requests - 1):
            start = start + jnp.where(i < r, new_len_ref[0, i], 0)
        end = start + new_len_ref[0, r]

        @pl.when((start < (j + 1) * TILE) & (end > j * TILE))
        def _():
            q = q_s[j]
            rows = pl.ds(pl.multiple_of(r * slots, slots), slots)
            s1 = lax.dot_general(
                q, prefix_ref[rows, :HEAD_DIMENSION], nt, preferred_element_type=jnp.float32
            )
            s2 = lax.dot_general(
                q, kv_ref[:, :HEAD_DIMENSION], nt, preferred_element_type=jnp.float32
            )
            slot = lax.broadcasted_iota(jnp.int32, s1.shape, 1)
            s1 = jnp.where(slot < prefix_len_ref[0, r], s1 * scale, neg_large)
            token = j * TILE + lax.rem(lax.broadcasted_iota(jnp.int32, s2.shape, 0), TILE)
            key = lax.broadcasted_iota(jnp.int32, s2.shape, 1)
            s2 = jnp.where((key >= start) & (key <= token), s2 * scale, neg_large)
            top = jnp.maximum(
                jnp.max(s1, axis=1, keepdims=True), jnp.max(s2, axis=1, keepdims=True)
            )
            p1 = jnp.exp(s1 - top)
            p2 = jnp.exp(s2 - top)
            total = jnp.sum(p1, axis=1, keepdims=True) + jnp.sum(p2, axis=1, keepdims=True)
            inverse = 1.0 / total
            o = jnp.dot(
                (p1 * inverse).astype(jnp.bfloat16),
                prefix_ref[rows, HEAD_DIMENSION:],
                preferred_element_type=jnp.float32,
            ) + jnp.dot(
                (p2 * inverse).astype(jnp.bfloat16),
                kv_ref[:, HEAD_DIMENSION:],
                preferred_element_type=jnp.float32,
            )
            own = j * TILE + lax.rem(lax.broadcasted_iota(jnp.int32, o.shape, 0), TILE)
            mine = (own >= start) & (own < end)
            o_s[j] = jnp.where(mine, o, o_s[j])

        return 0

    lax.fori_loop(0, tiles * requests, body, 0)
    per_tile = TILE // ROWS
    for p in range(8):
        at = order_ref[p]
        tile, part = at // per_tile, at % per_tile
        for h in range(heads):
            x_ref[p * ROWS : (p + 1) * ROWS, h * HEAD_DIMENSION : (h + 1) * HEAD_DIMENSION] = o_s[
                tile, pl.ds(pl.multiple_of(h * TILE + part * ROWS, ROWS), ROWS), :
            ].astype(jnp.bfloat16)
    for c in range(w_s.shape[0]):
        weights(c).wait()
        y_s[c] = jnp.dot(x_ref[...], w_s[c], preferred_element_type=jnp.float32).astype(
            jnp.bfloat16
        )
        for p in range(8):
            written(c, p).start()
    for c in range(w_s.shape[0]):
        for p in range(8):
            written(c, p).wait()


def attend(order, new_len, prefix_len, q, kv, prefix, w):
    tokens, width = q.shape
    heads = width // HEAD_DIMENSION
    columns = w.shape[1]
    chunk = 2048
    work = 2 * tokens * heads * (MAXB * PAGE_TOKENS + tokens) * HEAD_DIMENSION * 2 * 2
    return pl.pallas_call(
        attention_kernel,
        out_shape=[pltpu.HBM((ROWS, columns), jnp.bfloat16)] * 8,
        in_specs=[SMEM, SMEM, SMEM, VMEM, VMEM, ANY, ANY],
        out_specs=[ANY] * 8,
        scratch_shapes=[
            pltpu.VMEM(prefix.shape, prefix.dtype),
            pltpu.VMEM((tokens, width), jnp.bfloat16),
            pltpu.VMEM((tokens // TILE, heads * TILE, HEAD_DIMENSION), jnp.bfloat16),
            pltpu.VMEM((tokens // TILE, heads * TILE, HEAD_DIMENSION), jnp.float32),
            pltpu.VMEM((columns // chunk, width, chunk), jnp.bfloat16),
            pltpu.VMEM((columns // chunk, tokens, chunk), jnp.bfloat16),
            pltpu.SemaphoreType.DMA((columns // chunk,)),
            pltpu.SemaphoreType.DMA((columns // chunk, 8)),
            pltpu.SemaphoreType.DMA,
        ],
        compiler_params=pltpu.CompilerParams(vmem_limit_bytes=28 * MIB),
        cost_estimate=pl.CostEstimate(
            flops=0, bytes_accessed=0, transcendentals=0
        ),
        name="attention",
    )(order, new_len, prefix_len, q, kv, in_hbm(prefix), in_hbm(w))


def copy_kernel(in_ref, out_ref):
    out_ref[...] = in_ref[...]


def copied(pages):
    block = (pages.shape[0] // 8,) + pages.shape[1:]
    spec = pl.BlockSpec(block, lambda i: (i,) + (0,) * (len(block) - 1))
    return pl.pallas_call(
        copy_kernel,
        grid=(8,),
        in_specs=[spec],
        out_specs=spec,
        out_shape=jax.ShapeDtypeStruct(pages.shape, pages.dtype),
        compiler_params=pltpu.CompilerParams(vmem_limit_bytes=16 * MIB),
        cost_estimate=pl.CostEstimate(flops=0, bytes_accessed=4 * pages.size, transcendentals=0),
        name="keep",
    )(pages)


def rotary_tables(angles):
    cosine, sine = jnp.cos(angles), jnp.sin(angles)
    return (
        jnp.concatenate([cosine, cosine], axis=1),
        jnp.concatenate([-sine, sine], axis=1),
    )


def page_tags(groups, me, requests):
    rows = requests * NB
    owners = groups[:, :rows]
    prefix, new_tokens, full_length = (
        groups[:, rows + i * requests : rows + (i + 1) * requests] for i in range(3)
    )
    block = jnp.arange(NB, dtype=jnp.int32)
    pages = jnp.where(
        full_length == prefix + new_tokens, (prefix + new_tokens) // PAGE_TOKENS, 0
    )
    sent = (block < pages[:, :, None]).reshape(-1, rows)
    number = jnp.where((owners == me) & sent, jnp.arange(1, rows + 1, dtype=jnp.int32), rows + 1)
    tags = []
    last = jnp.zeros((groups.shape[0], 1), jnp.int32)
    for _ in range(CAP):
        last = jnp.min(jnp.where(number > last, number, rows + 1), axis=1, keepdims=True)
        tags.append(jnp.where(last <= rows, last, 0))
    return jnp.concatenate(tags, axis=1)


def on_device(
    hidden_in,
    attn_gain,
    q_weight,
    key_weight_matrix,
    value_weight_matrix,
    o_weight,
    kv_pool,
    block_table,
    request_len,
    prefix_len,
    new_len,
    page_owner,
):
    n_section, n_tp, n_dec = (lax.axis_size(a) for a in ("section", "tp", "dec"))
    devices = n_section * n_tp * n_dec
    x = hidden_in[0]
    tokens = ROWS * n_tp
    normed = normalize(x, attn_gain)

    far = send(normed, 2, 0)
    near_z = send(normed, 0, 1)
    right = send(normed, 3, 0)
    left = send(normed, 1, 0)

    tp = lax.axis_index("tp")
    px, pz = tp // 2, tp % 2
    order = jnp.stack([((px + dx) % (n_tp // 2)) * 2 + (pz ^ dz) for dx, dz in PIECES]).astype(
        jnp.int32
    )

    prefix, new_tokens, full_length = prefix_len[0], new_len[0], request_len[0]
    owners = page_owner[0, :, 0]
    plain = jnp.concatenate([owners, prefix, new_tokens, full_length])
    near_z, owner_row = lax.optimization_barrier((near_z, owners[None, :]))
    right_z = send(near_z, 3, 0)
    left_z = send(near_z, 1, 0)
    plain, normed = lax.optimization_barrier((plain, normed))
    groups = lax.all_to_all(
        jnp.broadcast_to(plain, (n_section * n_dec,) + plain.shape),
        ("section", "dec"),
        split_axis=0,
        concat_axis=0,
        tiled=True,
    )
    groups, far = lax.optimization_barrier((groups, far))
    far_z = send(far, 0, 1)
    gathered = (normed, near_z, right, left, far, right_z, left_z, far_z)

    pool = kv_pool[0, :, :, 0, :]
    angles, buffer, prefix_pages, place, wq, wkv = prepare(
        devices,
        tokens,
        prefix_len,
        new_len,
        request_len,
        block_table[0],
        owner_row,
        pool,
        q_weight[0],
        key_weight_matrix[0],
        value_weight_matrix[0],
    )
    cos, sin = rotary_tables(angles)
    q, kv, buffer = project(order, place, gathered, wq, wkv, cos, sin, buffer)
    received_pages = lax.all_to_all(
        buffer.reshape(devices, CAP, PAGE_TOKENS, 2 * HEAD_DIMENSION),
        ("section", "tp", "dec"),
        split_axis=0,
        concat_axis=0,
        tiled=True,
    )

    parts = dict(
        zip(
            PIECES,
            attend(
                order,
                new_len,
                prefix_len,
                q,
                kv,
                prefix_pages.reshape(-1, 2 * HEAD_DIMENSION),
                o_weight[0],
            ),
        )
    )

    far_pair = send(parts[2, 1], 0, 1)
    from_left_z = send(parts[1, 1], 1, 0)
    from_right_z = send(parts[3, 1], 3, 0)

    from_left = send(parts[1, 0], 1, 0)
    from_right = send(parts[3, 0], 3, 0)

    def total(*terms):
        return sum(t.astype(jnp.float32) for t in terms)

    received_pages, far_pair, from_left_z, from_right_z = lax.optimization_barrier(
        (received_pages, far_pair, from_left_z, from_right_z)
    )
    from_far = send(total(parts[2, 0], far_pair).astype(jnp.bfloat16), 2, 0)
    from_z = send(total(parts[0, 1], from_left_z, from_right_z).astype(jnp.bfloat16), 0, 1)
    mixed = total(x, parts[0, 0], from_left, from_right, from_z, from_far).astype(jnp.bfloat16)
    passed = shifted(mixed, "section", 1)[None]
    kept = copied(received_pages)

    me = (lax.axis_index("section") * n_tp + tp) * n_dec + lax.axis_index("dec")
    received_tags = jnp.broadcast_to(
        page_tags(groups, me, prefix.shape[0]).reshape(n_section, 1, n_dec, CAP),
        (n_section, n_tp, n_dec, CAP),
    ).reshape(1, devices, CAP)
    return passed, kept[None, :, :, :, None, :], received_tags


def solution(mesh):
    in_specs = (
        P("section", ("dec", "tp"), None),
        P("section", None),
        P("section", None, "tp"),
        P("section", None, "tp"),
        P("section", None, "tp"),
        P("section", "tp", None),
        P("section", "dec", None, "tp", None),
        P("section", "dec", None),
        P("section", "dec"),
        P("section", "dec"),
        P("section", "dec"),
        P("section", "dec", None),
    )
    out_specs = (
        P("section", ("dec", "tp"), None),
        P(("section", "tp", "dec"), None, None, None, None, None),
        P(("section", "tp", "dec"), None, None),
    )
    return jax.shard_map(
        on_device, mesh=mesh, in_specs=in_specs, out_specs=out_specs, check_vma=False
    )
```

```python
import functools
import math

import jax
import jax.numpy as jnp
from jax import lax
from jax.experimental import pallas as pl
from jax.experimental.pallas import tpu as pltpu
from jax.sharding import PartitionSpec as P

HEAD_DIMENSION = 128
PAGE_TOKENS = 16
MAXB = 40
NB = 56
CAP = 3
SOON = 5
ROWS = 32

theta_base = 500000.0
eps_norm = 1e-05
neg_large = -1e30

MIB = 1 << 20
VMEM = pl.BlockSpec(memory_space=pltpu.VMEM)
SMEM = pl.BlockSpec(memory_space=pltpu.SMEM)
ANY = pl.BlockSpec(memory_space=pl.ANY)

PIECES = ((0, 0), (0, 1), (1, 0), (3, 0), (2, 0), (1, 1), (3, 1), (2, 1))


def tp_route(dx, dz, n_tp):
    nx = n_tp // 2
    return [(x * 2 + z, ((x + dx) % nx) * 2 + (z ^ dz)) for x in range(nx) for z in range(2)]


def send(block, dx, dz):
    return lax.ppermute(block, "tp", tp_route(dx, dz, lax.axis_size("tp")))


def shifted(block, axis, distance):
    count = lax.axis_size(axis)
    return lax.ppermute(block, axis, [((i - distance) % count, i) for i in range(count)])


def norm_kernel(x_ref, gain_ref, out_ref, x_s, gain_s, sems):
    copies = (
        pltpu.make_async_copy(x_ref, x_s, sems.at[0]),
        pltpu.make_async_copy(gain_ref, gain_s, sems.at[1]),
    )
    for copy in copies:
        copy.start()
    for copy in copies:
        copy.wait()
    x = x_s[...].astype(jnp.float32)
    scale = lax.rsqrt(jnp.mean(x * x, axis=-1, keepdims=True) + eps_norm)
    out_ref[...] = (x * scale * gain_s[...]).astype(jnp.bfloat16)


def in_hbm(array):
    return pltpu.with_memory_space_constraint(array, pltpu.HBM)


def in_vmem(array):
    return pltpu.with_memory_space_constraint(array, pltpu.VMEM)


def normalize(x, gain):
    return pl.pallas_call(
        norm_kernel,
        out_shape=jax.ShapeDtypeStruct(x.shape, jnp.bfloat16),
        in_specs=[ANY, ANY],
        out_specs=VMEM,
        scratch_shapes=[
            pltpu.VMEM(x.shape, x.dtype),
            pltpu.VMEM(gain.shape, gain.dtype),
            pltpu.SemaphoreType.DMA((2,)),
        ],
        compiler_params=pltpu.CompilerParams(vmem_limit_bytes=16 * MIB),
        cost_estimate=pl.CostEstimate(flops=4 * x.size, bytes_accessed=4 * x.size, transcendentals=0),
        name="norm",
    )(in_hbm(x), in_hbm(gain))


def project_rows(pieces, w_ref, acc_ref):
    depth = w_ref.shape[0]
    block = 2048
    for c in range(depth // block):
        cols = slice(c * block, (c + 1) * block)
        x = jnp.concatenate([p[:, cols] for p in pieces], axis=0)
        part = jnp.dot(x, w_ref[cols, :], preferred_element_type=jnp.float32)
        acc_ref[...] = part if c == 0 else acc_ref[...] + part


def rotate(v, cos, sin):
    return v * cos + pltpu.roll(v, HEAD_DIMENSION // 2, 1) * sin


def write_rows(order, first, count, acc_q, acc_kv, cos_ref, sin_ref, q_ref, kv_ref):
    heads = acc_q.shape[1] // HEAD_DIMENSION
    for p in range(count):
        rows = pl.ds(pl.multiple_of(order[first + p] * ROWS, ROWS), ROWS)
        here = slice(p * ROWS, (p + 1) * ROWS)
        cos, sin = cos_ref[rows, :], sin_ref[rows, :]
        kv_ref[rows, :HEAD_DIMENSION] = rotate(acc_kv[here, :HEAD_DIMENSION], cos, sin).astype(
            jnp.bfloat16
        )
        kv_ref[rows, HEAD_DIMENSION:] = acc_kv[here, HEAD_DIMENSION:].astype(jnp.bfloat16)
        for h in range(heads):
            cols = slice(h * HEAD_DIMENSION, (h + 1) * HEAD_DIMENSION)
            q_ref[rows, cols] = rotate(acc_q[here, cols], cos, sin).astype(jnp.bfloat16)


def first_kernel(order, *refs):
    pieces = refs[:SOON]
    wq, wkv, cos_ref, sin_ref, q_ref, kv_ref, acc_q, acc_kv = refs[SOON:]
    project_rows(pieces, wkv, acc_kv)
    project_rows(pieces, wq, acc_q)
    q_ref[...] = jnp.zeros_like(q_ref)
    kv_ref[...] = jnp.zeros_like(kv_ref)
    write_rows(order, 0, SOON, acc_q, acc_kv, cos_ref, sin_ref, q_ref, kv_ref)


def project_first(order, pieces, wq, wkv, cos, sin):
    depth, n_q = wq.shape
    n_kv = wkv.shape[1]
    tokens = 8 * ROWS
    rows = SOON * ROWS
    return pl.pallas_call(
        first_kernel,
        in_specs=[SMEM] + [VMEM] * (SOON + 4),
        out_specs=[VMEM, VMEM],
        out_shape=[
            jax.ShapeDtypeStruct((tokens, n_q), jnp.bfloat16),
            jax.ShapeDtypeStruct((tokens, n_kv), jnp.bfloat16),
        ],
        scratch_shapes=[
            pltpu.VMEM((rows, n_q), jnp.float32),
            pltpu.VMEM((rows, n_kv), jnp.float32),
        ],
        compiler_params=pltpu.CompilerParams(vmem_limit_bytes=12 * MIB),
        cost_estimate=pl.CostEstimate(
            flops=2 * rows * depth * (n_q + n_kv),
            bytes_accessed=2 * depth * (n_q + n_kv + rows),
            transcendentals=0,
        ),
        name="qkv_first",
    )(order, *pieces, in_vmem(wq), in_vmem(wkv), cos, sin)


def qkv_kernel(order, place, *refs):
    pieces = refs[: 8 - SOON]
    wq, wkv, cos_ref, sin_ref, q_in, kv_in, buffer_ref = refs[8 - SOON : 15 - SOON]
    q_ref, kv_ref, out_ref, acc_q, acc_kv, sems = refs[15 - SOON :]
    del buffer_ref
    slots = out_ref.shape[0]
    count = kv_ref.shape[0] // PAGE_TOKENS
    project_rows(pieces, wkv, acc_kv)
    project_rows(pieces, wq, acc_q)
    q_ref[...] = q_in[...]
    kv_ref[...] = kv_in[...]
    write_rows(order, SOON, 8 - SOON, acc_q, acc_kv, cos_ref, sin_ref, q_ref, kv_ref)

    def copy(i):
        return pltpu.make_async_copy(
            kv_ref.at[pl.ds(i * PAGE_TOKENS, PAGE_TOKENS), :],
            out_ref.at[jnp.minimum(place[0, i], slots - 1)],
            sems.at[i],
        )

    for i in range(count):
        @pl.when(place[0, i] < slots)
        def _():
            copy(i).start()

    for i in range(count):
        @pl.when(place[0, i] < slots)
        def _():
            copy(i).wait()


def project(order, place, pieces, wq, wkv, cos, sin, buffer):
    depth, n_q = wq.shape
    n_kv = wkv.shape[1]
    tokens = 8 * ROWS
    rows = (8 - SOON) * ROWS
    q, kv = project_first(order, pieces[:SOON], wq, wkv, cos, sin)
    return pl.pallas_call(
        qkv_kernel,
        in_specs=[SMEM, SMEM] + [VMEM] * (8 - SOON + 6) + [ANY],
        out_specs=[VMEM, VMEM, ANY],
        out_shape=[
            jax.ShapeDtypeStruct((tokens, n_q), jnp.bfloat16),
            jax.ShapeDtypeStruct((tokens, n_kv), jnp.bfloat16),
            pltpu.HBM(buffer.shape, buffer.dtype),
        ],
        scratch_shapes=[
            pltpu.VMEM((rows, n_q), jnp.float32),
            pltpu.VMEM((rows, n_kv), jnp.float32),
            pltpu.SemaphoreType.DMA((tokens // PAGE_TOKENS,)),
        ],
        input_output_aliases={16 - SOON: 2},
        compiler_params=pltpu.CompilerParams(vmem_limit_bytes=12 * MIB),
        cost_estimate=pl.CostEstimate(
            flops=2 * rows * depth * (n_q + n_kv),
            bytes_accessed=2 * depth * (n_q + n_kv + rows),
            transcendentals=0,
        ),
        name="qkv",
    )(order, place, *pieces[SOON:], in_vmem(wq), in_vmem(wkv), cos, sin, q, kv, buffer)


def prepare_kernel(
    devices,
    prefix_len_in,
    new_len_in,
    full_len_in,
    table_in,
    owner_in,
    pool_in,
    frequency_ref,
    wq_ref,
    wk_ref,
    wv_ref,
    angles_ref,
    buffer_ref,
    prefix_ref,
    place_ref,
    wq_out,
    wkv_out,
    prefix_len_ref,
    new_len_ref,
    full_len_ref,
    table_ref,
    owner_ref,
    pool_ref,
    take_v,
    take_s,
    sems,
):
    pairs = (
        (prefix_len_in, prefix_len_ref),
        (new_len_in, new_len_ref),
        (full_len_in, full_len_ref),
        (table_in, table_ref),
        (owner_in, owner_ref),
        (pool_in, pool_ref),
        (wk_ref, wkv_out.at[:, pl.ds(0, HEAD_DIMENSION)]),
        (wv_ref, wkv_out.at[:, pl.ds(HEAD_DIMENSION, HEAD_DIMENSION)]),
        (wq_ref, wq_out),
    )
    copies = [pltpu.make_async_copy(a, b, sems.at[i]) for i, (a, b) in enumerate(pairs)]
    for copy in copies:
        copy.start()
    for copy in copies[:5]:
        copy.wait()

    requests = prefix_len_ref.shape[1]
    rows = owner_ref.shape[1]
    old = [prefix_len_ref[0, r] // PAGE_TOKENS for r in range(requests)]
    new = [new_len_ref[0, r] // PAGE_TOKENS for r in range(requests)]
    open_ = [
        full_len_ref[0, r] != prefix_len_ref[0, r] + new_len_ref[0, r] for r in range(requests)
    ]
    base = [0]
    for r in range(requests - 1):
        base.append(base[r] + new[r])

    def by_request(row, values):
        out = jnp.full(row.shape, values[0], jnp.int32)
        for r in range(1, requests):
            out = jnp.where(row >= r * NB, values[r], out)
        return out

    def targets(row, owner):
        block = row - by_request(row, [r * NB for r in range(requests)])
        kept = by_request(row, [jnp.where(open_[r], 0, old[r] + new[r]) for r in range(requests)])
        return block, jnp.where(block < kept, owner, devices)

    row = lax.broadcasted_iota(jnp.int32, (rows, 1), 0)
    lane = lax.broadcasted_iota(jnp.int32, (1, rows), 1)
    owner = owner_ref[...]
    block, target = targets(
        row, jnp.sum(jnp.where(lane == row, owner, 0), axis=1, keepdims=True)
    )
    _, across = targets(lane, owner)
    rank = jnp.sum(
        jnp.where((across == target) & (lane < row), 1, 0), axis=1, keepdims=True
    )
    slots = buffer_ref.shape[0]
    code = jnp.where(target < devices, target * CAP + rank, slots)
    ages = by_request(row, old)
    first = by_request(row, [r * MAXB for r in range(requests)])
    source = jnp.where(block < ages, first + block + 1, 0)
    hit = code == lax.broadcasted_iota(jnp.int32, (1, slots), 1)
    take_v[...] = jnp.sum(jnp.where(hit, source, 0), axis=0, keepdims=True) - 1
    taken = pltpu.make_async_copy(take_v, take_s, sems.at[len(pairs)])
    taken.start()
    fresh = jnp.where(
        (block >= ages) & (block < by_request(row, [old[r] + new[r] for r in range(requests)])),
        by_request(row, base) + block - ages,
        -1,
    )
    number = lax.broadcasted_iota(jnp.int32, place_ref.shape, 1)
    place_ref[...] = jnp.sum(jnp.where(fresh == number, code, 0), axis=0, keepdims=True)

    token = lax.broadcasted_iota(jnp.int32, (angles_ref.shape[0], 1), 0)
    shift = jnp.full(token.shape, prefix_len_ref[0, 0], jnp.int32)
    for r in range(1, requests):
        start = base[r] * PAGE_TOKENS
        shift = jnp.where(token >= start, prefix_len_ref[0, r] - start, shift)
    angles_ref[...] = (token + shift).astype(jnp.float32) * frequency_ref[...]

    copies[5].wait()

    def gather(i, _):
        prefix_ref[i] = pool_ref[table_ref[0, i]]
        return 0

    lax.fori_loop(0, prefix_ref.shape[0], gather, 0, unroll=8)
    taken.wait()

    def fill(i, _):
        at = take_s[0, i]
        page = pool_ref[table_ref[0, jnp.maximum(at, 0)]]
        buffer_ref[i] = jnp.where(at >= 0, page, jnp.zeros_like(page))
        return 0

    lax.fori_loop(0, slots, fill, 0, unroll=8)
    for copy in copies[6:]:
        copy.wait()


def prepare(
    devices, tokens, prefix_len, new_len, full_len, table, owner, pool, wq, wk, wv
):
    slots = devices * CAP
    half = HEAD_DIMENSION // 2
    frequency = theta_base ** (-(jnp.arange(half, dtype=jnp.float32) * 2.0) / HEAD_DIMENSION)
    depth = wq.shape[0]
    return pl.pallas_call(
        functools.partial(prepare_kernel, devices),
        out_shape=[
            jax.ShapeDtypeStruct((tokens, half), jnp.float32),
            pltpu.HBM((slots,) + pool.shape[1:], pool.dtype),
            jax.ShapeDtypeStruct((table.shape[1],) + pool.shape[1:], pool.dtype),
            jax.ShapeDtypeStruct((1, 128), jnp.int32),
            pltpu.VMEM(wq.shape, wq.dtype),
            pltpu.VMEM((depth, 2 * HEAD_DIMENSION), wk.dtype),
        ],
        in_specs=[ANY] * 6 + [VMEM] + [ANY] * 3,
        out_specs=[VMEM] * 6,
        scratch_shapes=[
            pltpu.SMEM(prefix_len.shape, jnp.int32),
            pltpu.SMEM(new_len.shape, jnp.int32),
            pltpu.SMEM(full_len.shape, jnp.int32),
            pltpu.SMEM(table.shape, jnp.int32),
            pltpu.VMEM(owner.shape, jnp.int32),
            pltpu.VMEM(pool.shape, pool.dtype),
            pltpu.VMEM((1, slots), jnp.int32),
            pltpu.SMEM((1, slots), jnp.int32),
            pltpu.SemaphoreType.DMA((10,)),
        ],
        compiler_params=pltpu.CompilerParams(vmem_limit_bytes=16 * MIB),
        cost_estimate=pl.CostEstimate(flops=0, bytes_accessed=20 * MIB, transcendentals=0),
        name="prepare",
    )(
        in_hbm(prefix_len),
        in_hbm(new_len),
        in_hbm(full_len),
        in_hbm(table),
        in_hbm(owner),
        in_hbm(pool),
        frequency[None, :],
        in_hbm(wq),
        in_hbm(wk),
        in_hbm(wv),
    )


TILE = 64


def attention_kernel(
    order_ref, new_len_ref, prefix_len_ref, q_ref, kv_ref, prefix_in, w_ref, *rest
):
    outs, (prefix_ref, x_ref, q_s, o_s, w_s, y_s, sems, out_sems, prefix_sem) = rest[:8], rest[8:]
    prefix_copy = pltpu.make_async_copy(prefix_in, prefix_ref, prefix_sem)
    prefix_copy.start()
    chunk = w_s.shape[2]

    def weights(c):
        return pltpu.make_async_copy(w_ref.at[:, pl.ds(c * chunk, chunk)], w_s.at[c], sems.at[c])

    def written(c, p):
        return pltpu.make_async_copy(
            y_s.at[c, pl.ds(p * ROWS, ROWS), :],
            outs[p].at[:, pl.ds(c * chunk, chunk)],
            out_sems.at[c, p],
        )


    tokens = q_ref.shape[0]
    heads = q_ref.shape[1] // HEAD_DIMENSION
    tiles = tokens // TILE
    requests = new_len_ref.shape[1]
    slots = MAXB * PAGE_TOKENS
    for j in range(tiles):
        for h in range(heads):
            q_s[j, h * TILE : (h + 1) * TILE, :] = q_ref[
                j * TILE : (j + 1) * TILE, h * HEAD_DIMENSION : (h + 1) * HEAD_DIMENSION
            ]
    prefix_copy.wait()
    for c in range(w_s.shape[0]):
        weights(c).start()
    scale = 1.0 / math.sqrt(HEAD_DIMENSION)
    nt = (((1,), (1,)), ((), ()))

    def body(i, _):
        j, r = i // requests, i % requests
        start = 0
        for i in range(requests - 1):
            start = start + jnp.where(i < r, new_len_ref[0, i], 0)
        end = start + new_len_ref[0, r]

        @pl.when((start < (j + 1) * TILE) & (end > j * TILE))
        def _():
            q = q_s[j]
            rows = pl.ds(pl.multiple_of(r * slots, slots), slots)
            s1 = lax.dot_general(
                q, prefix_ref[rows, :HEAD_DIMENSION], nt, preferred_element_type=jnp.float32
            )
            s2 = lax.dot_general(
                q, kv_ref[:, :HEAD_DIMENSION], nt, preferred_element_type=jnp.float32
            )
            slot = lax.broadcasted_iota(jnp.int32, s1.shape, 1)
            s1 = jnp.where(slot < prefix_len_ref[0, r], s1 * scale, neg_large)
            token = j * TILE + lax.rem(lax.broadcasted_iota(jnp.int32, s2.shape, 0), TILE)
            key = lax.broadcasted_iota(jnp.int32, s2.shape, 1)
            s2 = jnp.where((key >= start) & (key <= token), s2 * scale, neg_large)
            top = jnp.maximum(
                jnp.max(s1, axis=1, keepdims=True), jnp.max(s2, axis=1, keepdims=True)
            )
            p1 = jnp.exp(s1 - top)
            p2 = jnp.exp(s2 - top)
            total = jnp.sum(p1, axis=1, keepdims=True) + jnp.sum(p2, axis=1, keepdims=True)
            inverse = 1.0 / total
            o = jnp.dot(
                (p1 * inverse).astype(jnp.bfloat16),
                prefix_ref[rows, HEAD_DIMENSION:],
                preferred_element_type=jnp.float32,
            ) + jnp.dot(
                (p2 * inverse).astype(jnp.bfloat16),
                kv_ref[:, HEAD_DIMENSION:],
                preferred_element_type=jnp.float32,
            )
            own = j * TILE + lax.rem(lax.broadcasted_iota(jnp.int32, o.shape, 0), TILE)
            mine = (own >= start) & (own < end)
            o_s[j] = jnp.where(mine, o, o_s[j])

        return 0

    lax.fori_loop(0, tiles * requests, body, 0)
    per_tile = TILE // ROWS
    for p in range(8):
        at = order_ref[p]
        tile, part = at // per_tile, at % per_tile
        for h in range(heads):
            x_ref[p * ROWS : (p + 1) * ROWS, h * HEAD_DIMENSION : (h + 1) * HEAD_DIMENSION] = o_s[
                tile, pl.ds(pl.multiple_of(h * TILE + part * ROWS, ROWS), ROWS), :
            ].astype(jnp.bfloat16)
    for c in range(w_s.shape[0]):
        weights(c).wait()
        y_s[c] = jnp.dot(x_ref[...], w_s[c], preferred_element_type=jnp.float32).astype(
            jnp.bfloat16
        )
        for p in range(8):
            written(c, p).start()
    for c in range(w_s.shape[0]):
        for p in range(8):
            written(c, p).wait()


def attend(order, new_len, prefix_len, q, kv, prefix, w):
    tokens, width = q.shape
    heads = width // HEAD_DIMENSION
    columns = w.shape[1]
    chunk = 2048
    work = 2 * tokens * heads * (MAXB * PAGE_TOKENS + tokens) * HEAD_DIMENSION * 2 * 2
    return pl.pallas_call(
        attention_kernel,
        out_shape=[pltpu.HBM((ROWS, columns), jnp.bfloat16)] * 8,
        in_specs=[SMEM, SMEM, SMEM, VMEM, VMEM, ANY, ANY],
        out_specs=[ANY] * 8,
        scratch_shapes=[
            pltpu.VMEM(prefix.shape, prefix.dtype),
            pltpu.VMEM((tokens, width), jnp.bfloat16),
            pltpu.VMEM((tokens // TILE, heads * TILE, HEAD_DIMENSION), jnp.bfloat16),
            pltpu.VMEM((tokens // TILE, heads * TILE, HEAD_DIMENSION), jnp.float32),
            pltpu.VMEM((columns // chunk, width, chunk), jnp.bfloat16),
            pltpu.VMEM((columns // chunk, tokens, chunk), jnp.bfloat16),
            pltpu.SemaphoreType.DMA((columns // chunk,)),
            pltpu.SemaphoreType.DMA((columns // chunk, 8)),
            pltpu.SemaphoreType.DMA,
        ],
        compiler_params=pltpu.CompilerParams(vmem_limit_bytes=28 * MIB),
        cost_estimate=pl.CostEstimate(
            flops=0, bytes_accessed=0, transcendentals=0
        ),
        name="attention",
    )(order, new_len, prefix_len, q, kv, in_hbm(prefix), in_hbm(w))


def copy_kernel(in_ref, out_ref):
    out_ref[...] = in_ref[...]


def copied(pages):
    block = (pages.shape[0] // 8,) + pages.shape[1:]
    spec = pl.BlockSpec(block, lambda i: (i,) + (0,) * (len(block) - 1))
    return pl.pallas_call(
        copy_kernel,
        grid=(8,),
        in_specs=[spec],
        out_specs=spec,
        out_shape=jax.ShapeDtypeStruct(pages.shape, pages.dtype),
        compiler_params=pltpu.CompilerParams(vmem_limit_bytes=16 * MIB),
        cost_estimate=pl.CostEstimate(flops=0, bytes_accessed=4 * pages.size, transcendentals=0),
        name="keep",
    )(pages)


def rotary_tables(angles):
    cosine, sine = jnp.cos(angles), jnp.sin(angles)
    return (
        jnp.concatenate([cosine, cosine], axis=1),
        jnp.concatenate([-sine, sine], axis=1),
    )


def page_tags(groups, me, requests):
    rows = requests * NB
    owners = groups[:, :rows]
    prefix, new_tokens, full_length = (
        groups[:, rows + i * requests : rows + (i + 1) * requests] for i in range(3)
    )
    block = jnp.arange(NB, dtype=jnp.int32)
    pages = jnp.where(
        full_length == prefix + new_tokens, (prefix + new_tokens) // PAGE_TOKENS, 0
    )
    sent = (block < pages[:, :, None]).reshape(-1, rows)
    number = jnp.where((owners == me) & sent, jnp.arange(1, rows + 1, dtype=jnp.int32), rows + 1)
    tags = []
    last = jnp.zeros((groups.shape[0], 1), jnp.int32)
    for _ in range(CAP):
        last = jnp.min(jnp.where(number > last, number, rows + 1), axis=1, keepdims=True)
        tags.append(jnp.where(last <= rows, last, 0))
    return jnp.concatenate(tags, axis=1)


def on_device(
    hidden_in,
    attn_gain,
    q_weight,
    key_weight_matrix,
    value_weight_matrix,
    o_weight,
    kv_pool,
    block_table,
    request_len,
    prefix_len,
    new_len,
    page_owner,
):
    n_section, n_tp, n_dec = (lax.axis_size(a) for a in ("section", "tp", "dec"))
    devices = n_section * n_tp * n_dec
    x = hidden_in[0]
    tokens = ROWS * n_tp
    normed = normalize(x, attn_gain)

    far = send(normed, 2, 0)
    near_z = send(normed, 0, 1)
    right = send(normed, 3, 0)
    left = send(normed, 1, 0)

    tp = lax.axis_index("tp")
    px, pz = tp // 2, tp % 2
    order = jnp.stack([((px + dx) % (n_tp // 2)) * 2 + (pz ^ dz) for dx, dz in PIECES]).astype(
        jnp.int32
    )

    prefix, new_tokens, full_length = prefix_len[0], new_len[0], request_len[0]
    owners = page_owner[0, :, 0]
    plain = jnp.concatenate([owners, prefix, new_tokens, full_length])
    near_z, owner_row = lax.optimization_barrier((near_z, owners[None, :]))
    right_z = send(near_z, 3, 0)
    left_z = send(near_z, 1, 0)
    plain, normed = lax.optimization_barrier((plain, normed))
    groups = lax.all_to_all(
        jnp.broadcast_to(plain, (n_section * n_dec,) + plain.shape),
        ("section", "dec"),
        split_axis=0,
        concat_axis=0,
        tiled=True,
    )
    groups, far = lax.optimization_barrier((groups, far))
    far_z = send(far, 0, 1)
    gathered = (normed, near_z, right, left, far, right_z, left_z, far_z)

    pool = kv_pool[0, :, :, 0, :]
    angles, buffer, prefix_pages, place, wq, wkv = prepare(
        devices,
        tokens,
        prefix_len,
        new_len,
        request_len,
        block_table[0],
        owner_row,
        pool,
        q_weight[0],
        key_weight_matrix[0],
        value_weight_matrix[0],
    )
    cos, sin = rotary_tables(angles)
    q, kv, buffer = project(order, place, gathered, wq, wkv, cos, sin, buffer)
    received_pages = lax.all_to_all(
        buffer.reshape(devices, CAP, PAGE_TOKENS, 2 * HEAD_DIMENSION),
        ("section", "tp", "dec"),
        split_axis=0,
        concat_axis=0,
        tiled=True,
    )

    parts = dict(
        zip(
            PIECES,
            attend(
                order,
                new_len,
                prefix_len,
                q,
                kv,
                prefix_pages.reshape(-1, 2 * HEAD_DIMENSION),
                o_weight[0],
            ),
        )
    )

    far_pair = send(parts[2, 1], 0, 1)
    from_left_z = send(parts[1, 1], 1, 0)
    from_right_z = send(parts[3, 1], 3, 0)

    from_left = send(parts[1, 0], 1, 0)
    from_right = send(parts[3, 0], 3, 0)

    def total(*terms):
        return sum(t.astype(jnp.float32) for t in terms)

    received_pages, far_pair, from_left_z, from_right_z = lax.optimization_barrier(
        (received_pages, far_pair, from_left_z, from_right_z)
    )
    from_far = send(total(parts[2, 0], far_pair).astype(jnp.bfloat16), 2, 0)
    from_z = send(total(parts[0, 1], from_left_z, from_right_z).astype(jnp.bfloat16), 0, 1)
    ready = lax.optimization_barrier(total(x, parts[0, 0], from_left, from_right))
    mixed = total(ready, from_z, from_far).astype(jnp.bfloat16)
    passed = shifted(mixed, "section", 1)[None]
    kept = copied(received_pages)

    me = (lax.axis_index("section") * n_tp + tp) * n_dec + lax.axis_index("dec")
    received_tags = jnp.broadcast_to(
        page_tags(groups, me, prefix.shape[0]).reshape(n_section, 1, n_dec, CAP),
        (n_section, n_tp, n_dec, CAP),
    ).reshape(1, devices, CAP)
    return passed, kept[None, :, :, :, None, :], received_tags


def solution(mesh):
    in_specs = (
        P("section", ("dec", "tp"), None),
        P("section", None),
        P("section", None, "tp"),
        P("section", None, "tp"),
        P("section", None, "tp"),
        P("section", "tp", None),
        P("section", "dec", None, "tp", None),
        P("section", "dec", None),
        P("section", "dec"),
        P("section", "dec"),
        P("section", "dec"),
        P("section", "dec", None),
    )
    out_specs = (
        P("section", ("dec", "tp"), None),
        P(("section", "tp", "dec"), None, None, None, None, None),
        P(("section", "tp", "dec"), None, None),
    )
    return jax.shard_map(
        on_device, mesh=mesh, in_specs=in_specs, out_specs=out_specs, check_vma=False
    )
```

```python
import functools
import math

import jax
import jax.numpy as jnp
from jax import lax
from jax.experimental import pallas as pl
from jax.experimental.pallas import tpu as pltpu
from jax.sharding import PartitionSpec as P

HEAD_DIMENSION = 128
PAGE_TOKENS = 16
MAXB = 40
NB = 56
CAP = 3
SOON = 4
ROWS = 32

theta_base = 500000.0
eps_norm = 1e-05
neg_large = -1e30

MIB = 1 << 20
VMEM = pl.BlockSpec(memory_space=pltpu.VMEM)
SMEM = pl.BlockSpec(memory_space=pltpu.SMEM)
ANY = pl.BlockSpec(memory_space=pl.ANY)

PIECES = ((0, 0), (0, 1), (1, 0), (3, 0), (2, 0), (1, 1), (3, 1), (2, 1))


def tp_route(dx, dz, n_tp):
    nx = n_tp // 2
    return [(x * 2 + z, ((x + dx) % nx) * 2 + (z ^ dz)) for x in range(nx) for z in range(2)]


def send(block, dx, dz):
    return lax.ppermute(block, "tp", tp_route(dx, dz, lax.axis_size("tp")))


def shifted(block, axis, distance):
    count = lax.axis_size(axis)
    return lax.ppermute(block, axis, [((i - distance) % count, i) for i in range(count)])


def norm_kernel(x_ref, gain_ref, out_ref, x_s, gain_s, sems):
    copies = (
        pltpu.make_async_copy(x_ref, x_s, sems.at[0]),
        pltpu.make_async_copy(gain_ref, gain_s, sems.at[1]),
    )
    for copy in copies:
        copy.start()
    for copy in copies:
        copy.wait()
    x = x_s[...].astype(jnp.float32)
    scale = lax.rsqrt(jnp.mean(x * x, axis=-1, keepdims=True) + eps_norm)
    out_ref[...] = (x * scale * gain_s[...]).astype(jnp.bfloat16)


def in_hbm(array):
    return pltpu.with_memory_space_constraint(array, pltpu.HBM)


def in_vmem(array):
    return pltpu.with_memory_space_constraint(array, pltpu.VMEM)


def normalize(x, gain):
    return pl.pallas_call(
        norm_kernel,
        out_shape=jax.ShapeDtypeStruct(x.shape, jnp.bfloat16),
        in_specs=[ANY, ANY],
        out_specs=VMEM,
        scratch_shapes=[
            pltpu.VMEM(x.shape, x.dtype),
            pltpu.VMEM(gain.shape, gain.dtype),
            pltpu.SemaphoreType.DMA((2,)),
        ],
        compiler_params=pltpu.CompilerParams(vmem_limit_bytes=16 * MIB),
        cost_estimate=pl.CostEstimate(flops=4 * x.size, bytes_accessed=4 * x.size, transcendentals=0),
        name="norm",
    )(in_hbm(x), in_hbm(gain))


def project_rows(pieces, w_ref, acc_ref):
    depth = w_ref.shape[0]
    block = 2048
    for c in range(depth // block):
        cols = slice(c * block, (c + 1) * block)
        x = jnp.concatenate([p[:, cols] for p in pieces], axis=0)
        part = jnp.dot(x, w_ref[cols, :], preferred_element_type=jnp.float32)
        acc_ref[...] = part if c == 0 else acc_ref[...] + part


def rotate(v, cos, sin):
    return v * cos + pltpu.roll(v, HEAD_DIMENSION // 2, 1) * sin


def write_rows(order, first, count, acc_q, acc_kv, cos_ref, sin_ref, q_ref, kv_ref):
    heads = acc_q.shape[1] // HEAD_DIMENSION
    for p in range(count):
        rows = pl.ds(pl.multiple_of(order[first + p] * ROWS, ROWS), ROWS)
        here = slice(p * ROWS, (p + 1) * ROWS)
        cos, sin = cos_ref[rows, :], sin_ref[rows, :]
        kv_ref[rows, :HEAD_DIMENSION] = rotate(acc_kv[here, :HEAD_DIMENSION], cos, sin).astype(
            jnp.bfloat16
        )
        kv_ref[rows, HEAD_DIMENSION:] = acc_kv[here, HEAD_DIMENSION:].astype(jnp.bfloat16)
        for h in range(heads):
            cols = slice(h * HEAD_DIMENSION, (h + 1) * HEAD_DIMENSION)
            q_ref[rows, cols] = rotate(acc_q[here, cols], cos, sin).astype(jnp.bfloat16)


def first_kernel(order, *refs):
    pieces = refs[:SOON]
    wq, wkv, cos_ref, sin_ref, q_ref, kv_ref, acc_q, acc_kv = refs[SOON:]
    project_rows(pieces, wkv, acc_kv)
    project_rows(pieces, wq, acc_q)
    q_ref[...] = jnp.zeros_like(q_ref)
    kv_ref[...] = jnp.zeros_like(kv_ref)
    write_rows(order, 0, SOON, acc_q, acc_kv, cos_ref, sin_ref, q_ref, kv_ref)


def project_first(order, pieces, wq, wkv, cos, sin):
    depth, n_q = wq.shape
    n_kv = wkv.shape[1]
    tokens = 8 * ROWS
    rows = SOON * ROWS
    return pl.pallas_call(
        first_kernel,
        in_specs=[SMEM] + [VMEM] * (SOON + 4),
        out_specs=[VMEM, VMEM],
        out_shape=[
            jax.ShapeDtypeStruct((tokens, n_q), jnp.bfloat16),
            jax.ShapeDtypeStruct((tokens, n_kv), jnp.bfloat16),
        ],
        scratch_shapes=[
            pltpu.VMEM((rows, n_q), jnp.float32),
            pltpu.VMEM((rows, n_kv), jnp.float32),
        ],
        compiler_params=pltpu.CompilerParams(vmem_limit_bytes=12 * MIB),
        cost_estimate=pl.CostEstimate(
            flops=2 * rows * depth * (n_q + n_kv),
            bytes_accessed=2 * depth * (n_q + n_kv + rows),
            transcendentals=0,
        ),
        name="qkv_first",
    )(order, *pieces, in_vmem(wq), in_vmem(wkv), cos, sin)


def qkv_kernel(order, place, *refs):
    pieces = refs[: 8 - SOON]
    wq, wkv, cos_ref, sin_ref, q_in, kv_in, buffer_ref = refs[8 - SOON : 15 - SOON]
    q_ref, kv_ref, out_ref, acc_q, acc_kv, sems = refs[15 - SOON :]
    del buffer_ref
    slots = out_ref.shape[0]
    count = kv_ref.shape[0] // PAGE_TOKENS
    project_rows(pieces, wkv, acc_kv)
    project_rows(pieces, wq, acc_q)
    q_ref[...] = q_in[...]
    kv_ref[...] = kv_in[...]
    write_rows(order, SOON, 8 - SOON, acc_q, acc_kv, cos_ref, sin_ref, q_ref, kv_ref)

    def copy(i):
        return pltpu.make_async_copy(
            kv_ref.at[pl.ds(i * PAGE_TOKENS, PAGE_TOKENS), :],
            out_ref.at[jnp.minimum(place[0, i], slots - 1)],
            sems.at[i],
        )

    for i in range(count):
        @pl.when(place[0, i] < slots)
        def _():
            copy(i).start()

    for i in range(count):
        @pl.when(place[0, i] < slots)
        def _():
            copy(i).wait()


def project(order, place, pieces, wq, wkv, cos, sin, buffer):
    depth, n_q = wq.shape
    n_kv = wkv.shape[1]
    tokens = 8 * ROWS
    rows = (8 - SOON) * ROWS
    q, kv = project_first(order, pieces[:SOON], wq, wkv, cos, sin)
    return pl.pallas_call(
        qkv_kernel,
        in_specs=[SMEM, SMEM] + [VMEM] * (8 - SOON + 6) + [ANY],
        out_specs=[VMEM, VMEM, ANY],
        out_shape=[
            jax.ShapeDtypeStruct((tokens, n_q), jnp.bfloat16),
            jax.ShapeDtypeStruct((tokens, n_kv), jnp.bfloat16),
            pltpu.HBM(buffer.shape, buffer.dtype),
        ],
        scratch_shapes=[
            pltpu.VMEM((rows, n_q), jnp.float32),
            pltpu.VMEM((rows, n_kv), jnp.float32),
            pltpu.SemaphoreType.DMA((tokens // PAGE_TOKENS,)),
        ],
        input_output_aliases={16 - SOON: 2},
        compiler_params=pltpu.CompilerParams(vmem_limit_bytes=12 * MIB),
        cost_estimate=pl.CostEstimate(
            flops=2 * rows * depth * (n_q + n_kv),
            bytes_accessed=2 * depth * (n_q + n_kv + rows),
            transcendentals=0,
        ),
        name="qkv",
    )(order, place, *pieces[SOON:], in_vmem(wq), in_vmem(wkv), cos, sin, q, kv, buffer)


def prepare_kernel(
    devices,
    prefix_len_in,
    new_len_in,
    full_len_in,
    table_in,
    owner_in,
    pool_in,
    frequency_ref,
    wq_ref,
    wk_ref,
    wv_ref,
    angles_ref,
    buffer_ref,
    prefix_ref,
    place_ref,
    wq_out,
    wkv_out,
    prefix_len_ref,
    new_len_ref,
    full_len_ref,
    table_ref,
    owner_ref,
    pool_ref,
    take_v,
    take_s,
    sems,
):
    pairs = (
        (prefix_len_in, prefix_len_ref),
        (new_len_in, new_len_ref),
        (full_len_in, full_len_ref),
        (table_in, table_ref),
        (owner_in, owner_ref),
        (pool_in, pool_ref),
        (wk_ref, wkv_out.at[:, pl.ds(0, HEAD_DIMENSION)]),
        (wv_ref, wkv_out.at[:, pl.ds(HEAD_DIMENSION, HEAD_DIMENSION)]),
        (wq_ref, wq_out),
    )
    copies = [pltpu.make_async_copy(a, b, sems.at[i]) for i, (a, b) in enumerate(pairs)]
    for copy in copies:
        copy.start()
    for copy in copies[:5]:
        copy.wait()

    requests = prefix_len_ref.shape[1]
    rows = owner_ref.shape[1]
    old = [prefix_len_ref[0, r] // PAGE_TOKENS for r in range(requests)]
    new = [new_len_ref[0, r] // PAGE_TOKENS for r in range(requests)]
    open_ = [
        full_len_ref[0, r] != prefix_len_ref[0, r] + new_len_ref[0, r] for r in range(requests)
    ]
    base = [0]
    for r in range(requests - 1):
        base.append(base[r] + new[r])

    def by_request(row, values):
        out = jnp.full(row.shape, values[0], jnp.int32)
        for r in range(1, requests):
            out = jnp.where(row >= r * NB, values[r], out)
        return out

    def targets(row, owner):
        block = row - by_request(row, [r * NB for r in range(requests)])
        kept = by_request(row, [jnp.where(open_[r], 0, old[r] + new[r]) for r in range(requests)])
        return block, jnp.where(block < kept, owner, devices)

    row = lax.broadcasted_iota(jnp.int32, (rows, 1), 0)
    lane = lax.broadcasted_iota(jnp.int32, (1, rows), 1)
    owner = owner_ref[...]
    block, target = targets(
        row, jnp.sum(jnp.where(lane == row, owner, 0), axis=1, keepdims=True)
    )
    _, across = targets(lane, owner)
    rank = jnp.sum(
        jnp.where((across == target) & (lane < row), 1, 0), axis=1, keepdims=True
    )
    slots = buffer_ref.shape[0]
    code = jnp.where(target < devices, target * CAP + rank, slots)
    ages = by_request(row, old)
    first = by_request(row, [r * MAXB for r in range(requests)])
    source = jnp.where(block < ages, first + block + 1, 0)
    hit = code == lax.broadcasted_iota(jnp.int32, (1, slots), 1)
    take_v[...] = jnp.sum(jnp.where(hit, source, 0), axis=0, keepdims=True) - 1
    taken = pltpu.make_async_copy(take_v, take_s, sems.at[len(pairs)])
    taken.start()
    fresh = jnp.where(
        (block >= ages) & (block < by_request(row, [old[r] + new[r] for r in range(requests)])),
        by_request(row, base) + block - ages,
        -1,
    )
    number = lax.broadcasted_iota(jnp.int32, place_ref.shape, 1)
    place_ref[...] = jnp.sum(jnp.where(fresh == number, code, 0), axis=0, keepdims=True)

    token = lax.broadcasted_iota(jnp.int32, (angles_ref.shape[0], 1), 0)
    shift = jnp.full(token.shape, prefix_len_ref[0, 0], jnp.int32)
    for r in range(1, requests):
        start = base[r] * PAGE_TOKENS
        shift = jnp.where(token >= start, prefix_len_ref[0, r] - start, shift)
    angles_ref[...] = (token + shift).astype(jnp.float32) * frequency_ref[...]

    copies[5].wait()

    def gather(i, _):
        prefix_ref[i] = pool_ref[table_ref[0, i]]
        return 0

    lax.fori_loop(0, prefix_ref.shape[0], gather, 0, unroll=8)
    taken.wait()

    def fill(i, _):
        at = take_s[0, i]
        page = pool_ref[table_ref[0, jnp.maximum(at, 0)]]
        buffer_ref[i] = jnp.where(at >= 0, page, jnp.zeros_like(page))
        return 0

    lax.fori_loop(0, slots, fill, 0, unroll=8)
    for copy in copies[6:]:
        copy.wait()


def prepare(
    devices, tokens, prefix_len, new_len, full_len, table, owner, pool, wq, wk, wv
):
    slots = devices * CAP
    half = HEAD_DIMENSION // 2
    frequency = theta_base ** (-(jnp.arange(half, dtype=jnp.float32) * 2.0) / HEAD_DIMENSION)
    depth = wq.shape[0]
    return pl.pallas_call(
        functools.partial(prepare_kernel, devices),
        out_shape=[
            jax.ShapeDtypeStruct((tokens, half), jnp.float32),
            pltpu.HBM((slots,) + pool.shape[1:], pool.dtype),
            jax.ShapeDtypeStruct((table.shape[1],) + pool.shape[1:], pool.dtype),
            jax.ShapeDtypeStruct((1, 128), jnp.int32),
            pltpu.VMEM(wq.shape, wq.dtype),
            pltpu.VMEM((depth, 2 * HEAD_DIMENSION), wk.dtype),
        ],
        in_specs=[ANY] * 6 + [VMEM] + [ANY] * 3,
        out_specs=[VMEM] * 6,
        scratch_shapes=[
            pltpu.SMEM(prefix_len.shape, jnp.int32),
            pltpu.SMEM(new_len.shape, jnp.int32),
            pltpu.SMEM(full_len.shape, jnp.int32),
            pltpu.SMEM(table.shape, jnp.int32),
            pltpu.VMEM(owner.shape, jnp.int32),
            pltpu.VMEM(pool.shape, pool.dtype),
            pltpu.VMEM((1, slots), jnp.int32),
            pltpu.SMEM((1, slots), jnp.int32),
            pltpu.SemaphoreType.DMA((10,)),
        ],
        compiler_params=pltpu.CompilerParams(vmem_limit_bytes=16 * MIB),
        cost_estimate=pl.CostEstimate(flops=0, bytes_accessed=20 * MIB, transcendentals=0),
        name="prepare",
    )(
        in_hbm(prefix_len),
        in_hbm(new_len),
        in_hbm(full_len),
        in_hbm(table),
        in_hbm(owner),
        in_hbm(pool),
        frequency[None, :],
        in_hbm(wq),
        in_hbm(wk),
        in_hbm(wv),
    )


TILE = 64


def attention_kernel(
    order_ref, new_len_ref, prefix_len_ref, q_ref, kv_ref, prefix_in, w_ref, *rest
):
    outs, (prefix_ref, x_ref, q_s, o_s, w_s, y_s, sems, out_sems, prefix_sem) = rest[:8], rest[8:]
    prefix_copy = pltpu.make_async_copy(prefix_in, prefix_ref, prefix_sem)
    prefix_copy.start()
    chunk = w_s.shape[2]

    def weights(c):
        return pltpu.make_async_copy(w_ref.at[:, pl.ds(c * chunk, chunk)], w_s.at[c], sems.at[c])

    def written(c, p):
        return pltpu.make_async_copy(
            y_s.at[c, pl.ds(p * ROWS, ROWS), :],
            outs[p].at[:, pl.ds(c * chunk, chunk)],
            out_sems.at[c, p],
        )


    tokens = q_ref.shape[0]
    heads = q_ref.shape[1] // HEAD_DIMENSION
    tiles = tokens // TILE
    requests = new_len_ref.shape[1]
    slots = MAXB * PAGE_TOKENS
    for j in range(tiles):
        for h in range(heads):
            q_s[j, h * TILE : (h + 1) * TILE, :] = q_ref[
                j * TILE : (j + 1) * TILE, h * HEAD_DIMENSION : (h + 1) * HEAD_DIMENSION
            ]
    prefix_copy.wait()
    for c in range(w_s.shape[0]):
        weights(c).start()
    scale = 1.0 / math.sqrt(HEAD_DIMENSION)
    nt = (((1,), (1,)), ((), ()))

    def body(i, _):
        j, r = i // requests, i % requests
        start = 0
        for i in range(requests - 1):
            start = start + jnp.where(i < r, new_len_ref[0, i], 0)
        end = start + new_len_ref[0, r]

        @pl.when((start < (j + 1) * TILE) & (end > j * TILE))
        def _():
            q = q_s[j]
            rows = pl.ds(pl.multiple_of(r * slots, slots), slots)
            s1 = lax.dot_general(
                q, prefix_ref[rows, :HEAD_DIMENSION], nt, preferred_element_type=jnp.float32
            )
            s2 = lax.dot_general(
                q, kv_ref[:, :HEAD_DIMENSION], nt, preferred_element_type=jnp.float32
            )
            slot = lax.broadcasted_iota(jnp.int32, s1.shape, 1)
            s1 = jnp.where(slot < prefix_len_ref[0, r], s1 * scale, neg_large)
            token = j * TILE + lax.rem(lax.broadcasted_iota(jnp.int32, s2.shape, 0), TILE)
            key = lax.broadcasted_iota(jnp.int32, s2.shape, 1)
            s2 = jnp.where((key >= start) & (key <= token), s2 * scale, neg_large)
            top = jnp.maximum(
                jnp.max(s1, axis=1, keepdims=True), jnp.max(s2, axis=1, keepdims=True)
            )
            p1 = jnp.exp(s1 - top)
            p2 = jnp.exp(s2 - top)
            total = jnp.sum(p1, axis=1, keepdims=True) + jnp.sum(p2, axis=1, keepdims=True)
            inverse = 1.0 / total
            o = jnp.dot(
                (p1 * inverse).astype(jnp.bfloat16),
                prefix_ref[rows, HEAD_DIMENSION:],
                preferred_element_type=jnp.float32,
            ) + jnp.dot(
                (p2 * inverse).astype(jnp.bfloat16),
                kv_ref[:, HEAD_DIMENSION:],
                preferred_element_type=jnp.float32,
            )
            own = j * TILE + lax.rem(lax.broadcasted_iota(jnp.int32, o.shape, 0), TILE)
            mine = (own >= start) & (own < end)
            o_s[j] = jnp.where(mine, o, o_s[j])

        return 0

    lax.fori_loop(0, tiles * requests, body, 0)
    per_tile = TILE // ROWS
    for p in range(8):
        at = order_ref[p]
        tile, part = at // per_tile, at % per_tile
        for h in range(heads):
            x_ref[p * ROWS : (p + 1) * ROWS, h * HEAD_DIMENSION : (h + 1) * HEAD_DIMENSION] = o_s[
                tile, pl.ds(pl.multiple_of(h * TILE + part * ROWS, ROWS), ROWS), :
            ].astype(jnp.bfloat16)
    for c in range(w_s.shape[0]):
        weights(c).wait()
        y_s[c] = jnp.dot(x_ref[...], w_s[c], preferred_element_type=jnp.float32).astype(
            jnp.bfloat16
        )
        for p in range(8):
            written(c, p).start()
    for c in range(w_s.shape[0]):
        for p in range(8):
            written(c, p).wait()


def attend(order, new_len, prefix_len, q, kv, prefix, w):
    tokens, width = q.shape
    heads = width // HEAD_DIMENSION
    columns = w.shape[1]
    chunk = 2048
    work = 2 * tokens * heads * (MAXB * PAGE_TOKENS + tokens) * HEAD_DIMENSION * 2 * 2
    return pl.pallas_call(
        attention_kernel,
        out_shape=[pltpu.HBM((ROWS, columns), jnp.bfloat16)] * 8,
        in_specs=[SMEM, SMEM, SMEM, VMEM, VMEM, ANY, ANY],
        out_specs=[ANY] * 8,
        scratch_shapes=[
            pltpu.VMEM(prefix.shape, prefix.dtype),
            pltpu.VMEM((tokens, width), jnp.bfloat16),
            pltpu.VMEM((tokens // TILE, heads * TILE, HEAD_DIMENSION), jnp.bfloat16),
            pltpu.VMEM((tokens // TILE, heads * TILE, HEAD_DIMENSION), jnp.float32),
            pltpu.VMEM((columns // chunk, width, chunk), jnp.bfloat16),
            pltpu.VMEM((columns // chunk, tokens, chunk), jnp.bfloat16),
            pltpu.SemaphoreType.DMA((columns // chunk,)),
            pltpu.SemaphoreType.DMA((columns // chunk, 8)),
            pltpu.SemaphoreType.DMA,
        ],
        compiler_params=pltpu.CompilerParams(vmem_limit_bytes=28 * MIB),
        cost_estimate=pl.CostEstimate(
            flops=0, bytes_accessed=0, transcendentals=0
        ),
        name="attention",
    )(order, new_len, prefix_len, q, kv, in_hbm(prefix), in_hbm(w))


def copy_kernel(in_ref, out_ref):
    out_ref[...] = in_ref[...]


def copied(pages):
    block = (pages.shape[0] // 8,) + pages.shape[1:]
    spec = pl.BlockSpec(block, lambda i: (i,) + (0,) * (len(block) - 1))
    return pl.pallas_call(
        copy_kernel,
        grid=(8,),
        in_specs=[spec],
        out_specs=spec,
        out_shape=jax.ShapeDtypeStruct(pages.shape, pages.dtype),
        compiler_params=pltpu.CompilerParams(vmem_limit_bytes=16 * MIB),
        cost_estimate=pl.CostEstimate(flops=0, bytes_accessed=4 * pages.size, transcendentals=0),
        name="keep",
    )(pages)


def rotary_tables(angles):
    cosine, sine = jnp.cos(angles), jnp.sin(angles)
    return (
        jnp.concatenate([cosine, cosine], axis=1),
        jnp.concatenate([-sine, sine], axis=1),
    )


def page_tags(groups, me, requests):
    rows = requests * NB
    owners = groups[:, :rows]
    prefix, new_tokens, full_length = (
        groups[:, rows + i * requests : rows + (i + 1) * requests] for i in range(3)
    )
    block = jnp.arange(NB, dtype=jnp.int32)
    pages = jnp.where(
        full_length == prefix + new_tokens, (prefix + new_tokens) // PAGE_TOKENS, 0
    )
    sent = (block < pages[:, :, None]).reshape(-1, rows)
    number = jnp.where((owners == me) & sent, jnp.arange(1, rows + 1, dtype=jnp.int32), rows + 1)
    tags = []
    last = jnp.zeros((groups.shape[0], 1), jnp.int32)
    for _ in range(CAP):
        last = jnp.min(jnp.where(number > last, number, rows + 1), axis=1, keepdims=True)
        tags.append(jnp.where(last <= rows, last, 0))
    return jnp.concatenate(tags, axis=1)


def on_device(
    hidden_in,
    attn_gain,
    q_weight,
    key_weight_matrix,
    value_weight_matrix,
    o_weight,
    kv_pool,
    block_table,
    request_len,
    prefix_len,
    new_len,
    page_owner,
):
    n_section, n_tp, n_dec = (lax.axis_size(a) for a in ("section", "tp", "dec"))
    devices = n_section * n_tp * n_dec
    x = hidden_in[0]
    tokens = ROWS * n_tp
    normed = normalize(x, attn_gain)

    far = send(normed, 2, 0)
    near_z = send(normed, 0, 1)
    right = send(normed, 3, 0)
    left = send(normed, 1, 0)

    tp = lax.axis_index("tp")
    px, pz = tp // 2, tp % 2
    order = jnp.stack([((px + dx) % (n_tp // 2)) * 2 + (pz ^ dz) for dx, dz in PIECES]).astype(
        jnp.int32
    )

    prefix, new_tokens, full_length = prefix_len[0], new_len[0], request_len[0]
    owners = page_owner[0, :, 0]
    plain = jnp.concatenate([owners, prefix, new_tokens, full_length])
    near_z, owner_row = lax.optimization_barrier((near_z, owners[None, :]))
    right_z = send(near_z, 3, 0)
    left_z = send(near_z, 1, 0)
    plain, normed = lax.optimization_barrier((plain, normed))
    groups = lax.all_to_all(
        jnp.broadcast_to(plain, (n_section * n_dec,) + plain.shape),
        ("section", "dec"),
        split_axis=0,
        concat_axis=0,
        tiled=True,
    )
    groups, far = lax.optimization_barrier((groups, far))
    far_z = send(far, 0, 1)
    gathered = (normed, near_z, right, left, far, right_z, left_z, far_z)

    pool = kv_pool[0, :, :, 0, :]
    angles, buffer, prefix_pages, place, wq, wkv = prepare(
        devices,
        tokens,
        prefix_len,
        new_len,
        request_len,
        block_table[0],
        owner_row,
        pool,
        q_weight[0],
        key_weight_matrix[0],
        value_weight_matrix[0],
    )
    cos, sin = rotary_tables(angles)
    q, kv, buffer = project(order, place, gathered, wq, wkv, cos, sin, buffer)
    received_pages = lax.all_to_all(
        buffer.reshape(devices, CAP, PAGE_TOKENS, 2 * HEAD_DIMENSION),
        ("section", "tp", "dec"),
        split_axis=0,
        concat_axis=0,
        tiled=True,
    )

    parts = dict(
        zip(
            PIECES,
            attend(
                order,
                new_len,
                prefix_len,
                q,
                kv,
                prefix_pages.reshape(-1, 2 * HEAD_DIMENSION),
                o_weight[0],
            ),
        )
    )

    far_pair = send(parts[2, 1], 0, 1)
    from_left_z = send(parts[1, 1], 1, 0)
    from_right_z = send(parts[3, 1], 3, 0)

    from_left = send(parts[1, 0], 1, 0)
    from_right = send(parts[3, 0], 3, 0)

    def total(*terms):
        return sum(t.astype(jnp.float32) for t in terms)

    received_pages, far_pair, from_left_z, from_right_z = lax.optimization_barrier(
        (received_pages, far_pair, from_left_z, from_right_z)
    )
    from_far = send(total(parts[2, 0], far_pair).astype(jnp.bfloat16), 2, 0)
    from_z = send(total(parts[0, 1], from_left_z, from_right_z).astype(jnp.bfloat16), 0, 1)
    ready = lax.optimization_barrier(total(x, parts[0, 0], from_left, from_right))
    mixed = total(ready, from_z, from_far).astype(jnp.bfloat16)
    passed = shifted(mixed, "section", 1)[None]
    kept = copied(received_pages)

    me = (lax.axis_index("section") * n_tp + tp) * n_dec + lax.axis_index("dec")
    received_tags = jnp.broadcast_to(
        page_tags(groups, me, prefix.shape[0]).reshape(n_section, 1, n_dec, CAP),
        (n_section, n_tp, n_dec, CAP),
    ).reshape(1, devices, CAP)
    return passed, kept[None, :, :, :, None, :], received_tags


def solution(mesh):
    in_specs = (
        P("section", ("dec", "tp"), None),
        P("section", None),
        P("section", None, "tp"),
        P("section", None, "tp"),
        P("section", None, "tp"),
        P("section", "tp", None),
        P("section", "dec", None, "tp", None),
        P("section", "dec", None),
        P("section", "dec"),
        P("section", "dec"),
        P("section", "dec"),
        P("section", "dec", None),
    )
    out_specs = (
        P("section", ("dec", "tp"), None),
        P(("section", "tp", "dec"), None, None, None, None, None),
        P(("section", "tp", "dec"), None, None),
    )
    return jax.shard_map(
        on_device, mesh=mesh, in_specs=in_specs, out_specs=out_specs, check_vma=False
    )
```
